256 devices in a mesh: span: 32 (over x, y, core), band: 8 (over z).
Axes of the slice: x: 4, y: 4, z: 8, core: 2. Of those that a mesh axis runs over, the one named last changes fastest.
Arguments:
- start_block: float32 [524288, 128], P(('span', 'band')), may hold values from -500 to 500
- diagonal: float32 [524288], P(('span', 'band')), may hold values from 0.5 to 2
- blocks: bfloat16 [2048, 8, 256, 256], P(('span', 'band')), may hold values from -0.25 to 0.25
- span_offsets: int32 [2048, 8], P(('span', 'band')), may hold values from -1 to 1, as said below
- col_offsets: int32 [2048, 8], P(('span', 'band')), may hold values from -2 to 2
Outputs:
- bases_out: float32 [3, 524288, 128], P(None, ('span', 'band'))
- hessenberg: float32 [512, 384], replicated
- r_first: float32 [128, 128], replicated
The draws below stay inside these ranges and needn't reach their ends.
Inputs may be any that keep to these rules, and one draw needn't show every extreme that they name: The 8 pairs (span_offsets, col_offsets) of one block row are different from each other.
All inputs are finite; a program needn't handle non-finite values.
Results may differ from the reference program's by a relative error of at most 0.0029.
The reference program's roundings to bfloat16 on the way count: a program that leaves them out, or rounds other values in their place, can miss the bound.
Values may be sent and summed in bfloat16 or wider, within the bound.
A program may use at most 128 MiB of HBM per device.

```python
import math
import jax
import jax.numpy as jnp
from jax import lax

BS = 256
S = 128
K = 8
W = 2
STEPS = 3
SEG_BLOCKS = 64
NBLOCKS = 2048
NROWS = 524288
N_SPAN = 32


def draw_start_block(key, part):
    key_entry, key_column = jax.random.split(key, 2)
    row_place = jnp.arange(NROWS, dtype=jnp.float32) / NROWS
    entries = jnp.clip(jax.random.normal(key_entry, (NROWS, S), jnp.float32), -5.0, 5.0)
    column_scale = jnp.exp(jax.random.uniform(key_column, (1, S), jnp.float32, 0.0, math.log(10.0)))
    row_scale = jnp.exp(math.log(3.0) * row_place)[:, None]
    return entries * row_scale * column_scale


def pair_codes(key):
    row_keys = jax.random.split(jax.random.fold_in(key, 11), NBLOCKS)
    choose_pairs = jax.vmap(lambda one_key: jax.random.permutation(one_key, 3 * (2 * W + 1))[:K])
    return choose_pairs(row_keys).astype(jnp.int32)


def draw_span_offsets(key, part):
    return pair_codes(key) // (2 * W + 1) - 1


def draw_col_offsets(key, part):
    return pair_codes(key) % (2 * W + 1) - W


def block_scale(own_key, shape, cuts, least, high):
    loudness = 1.0
    for position, parts in cuts:
        draws = jax.random.uniform(jax.random.fold_in(jax.random.fold_in(own_key, 6), position), (parts,), jnp.float32, least / len(cuts), high / len(cuts))
        loudness = loudness * jnp.repeat(jnp.exp(draws), shape[position] // parts).reshape((-1,) + (1,) * (len(shape) - 1 - position))
    return loudness


def normal_values(key, extent, spread, most, cuts=(), kind=jnp.bfloat16):
    array = spread * jax.random.normal(key, extent, jnp.float32)
    if cuts:
        array = array * block_scale(key, extent, cuts, -0.22, 0.18)
    return jnp.clip(array, -most, most).astype(kind)


def setup_inputs(seed: int = 0) -> dict:
    key_list = jax.random.split(jax.random.key(seed), 6)
    start_block = draw_start_block(jax.random.fold_in(key_list[5], 71), 0)
    diagonal = jnp.clip(jnp.exp(math.log(2.0) - 1.3862944 * jax.random.uniform(key_list[1], (NROWS,), jnp.float32) ** block_scale(key_list[1], (NROWS,), ((0, 256),), -0.2, 0.2)), 0.5, 2.0)
    blocks = normal_values(key_list[2], (NBLOCKS, K, BS, BS), (K * BS // 4) ** -0.5, 0.25, ((0, 256),))
    span_offsets = draw_span_offsets(jax.random.fold_in(key_list[5], 71), 0)
    col_offsets = draw_col_offsets(jax.random.fold_in(key_list[5], 71), 0)
    return {"start_block": start_block, "diagonal": diagonal, "blocks": blocks, "span_offsets": span_offsets, "col_offsets": col_offsets}


def inner_product(first, second):
    return jnp.dot(first.T.astype(jnp.float32), second.astype(jnp.float32), precision=lax.Precision.HIGHEST, preferred_element_type=jnp.float32) / NROWS

def factor(matrix):
    gram_mat = inner_product(matrix, matrix)
    lower_fac = jnp.linalg.cholesky(gram_mat)
    identity = jnp.eye(S, dtype=jnp.float32)
    inverse = jax.scipy.linalg.solve_triangular(lower_fac, identity, lower=True)
    basis = jnp.dot(matrix.astype(jnp.float32), inverse.T.astype(jnp.float32), precision=lax.Precision.HIGHEST, preferred_element_type=jnp.float32)
    return (lower_fac.T, basis)

def apply_operator(vector, diagonal, blocks, span_offsets, col_offsets):
    lowered = vector.astype(jnp.bfloat16)
    extended = lowered.reshape(N_SPAN, SEG_BLOCKS, BS, S)
    extended = jnp.pad(extended, ((1, 1), (W, W), (0, 0), (0, 0)))
    seg_blocks = blocks.reshape(N_SPAN, SEG_BLOCKS, K, BS, BS)
    seg_spans = span_offsets.reshape(N_SPAN, SEG_BLOCKS, K)
    seg_cols = col_offsets.reshape(N_SPAN, SEG_BLOCKS, K)

    def one_segment(packed):
        segment, these_blocks, these_spans, these_cols = packed
        row_ids = jnp.arange(SEG_BLOCKS, dtype=jnp.int32)[:, None]
        span_index = (segment + 1 + these_spans).astype(jnp.int32)
        col_index = (row_ids + W + these_cols).astype(jnp.int32)
        picked = extended[span_index, col_index]
        return jnp.einsum('ikab,ikbc->iac', these_blocks.astype(jnp.float32), picked.astype(jnp.float32), precision=lax.Precision.HIGHEST)
    coupled = lax.map(one_segment, (jnp.arange(N_SPAN, dtype=jnp.int32), seg_blocks, seg_spans, seg_cols))
    return diagonal[:, None] * vector + coupled.reshape(NROWS, S)

def reference(start_block, diagonal, blocks, span_offsets, col_offsets):
    r_first, current = factor(start_block)
    bases = [current]
    columns = []
    for step_id in range(STEPS):
        mapped = apply_operator(bases[-1], diagonal, blocks, span_offsets, col_offsets)
        coeffs = [inner_product(earlier, mapped) for earlier in bases]
        residual = mapped
        for earlier, coeff_block in zip(bases, coeffs):
            residual = residual - jnp.dot(earlier.astype(jnp.float32), coeff_block.astype(jnp.float32), precision=lax.Precision.HIGHEST, preferred_element_type=jnp.float32)
        r_next, q_next = factor(residual)
        pieces = coeffs + [r_next]
        if STEPS - 1 - step_id > 0:
            pieces = pieces + [jnp.zeros(((STEPS - 1 - step_id) * S, S), jnp.float32)]
        columns.append(jnp.concatenate(pieces, axis=0))
        bases.append(q_next)
    hessenberg = jnp.concatenate(columns, axis=1)
    bases_out = jnp.stack(bases[1:])
    return (bases_out, hessenberg, r_first)
```

```python
import jax
import jax.numpy as jnp
from jax import lax
from jax.experimental import pallas as pl
from jax.experimental.pallas import tpu as pltpu
from jax.sharding import PartitionSpec as P

W = 2
STEPS = 3
LIMIT = 16384.0
F32 = jnp.float32
BF16 = jnp.bfloat16
MESH = pl.DeviceIdType.MESH
HIGHEST = lax.Precision.HIGHEST


def padded(block, sides, width):
    for axis, dim in sides:
        count = lax.axis_size(axis)
        forward = [(i, i + 1) for i in range(count - 1)]
        backward = [(target, source) for source, target in forward]
        low = lax.ppermute(
            lax.slice_in_dim(block, block.shape[dim] - width, None, axis=dim), axis, forward
        )
        high = lax.ppermute(lax.slice_in_dim(block, 0, width, axis=dim), axis, backward)
        block = jnp.concatenate([low, block, high], axis=dim)
    return block


def local_inner(first, second, row_total):
    return (
        jnp.dot(first.T, second, precision=HIGHEST, preferred_element_type=jnp.float32) / row_total
    )


def from_upper(upper_fac, matrix):
    identity = jnp.eye(upper_fac.shape[0], dtype=jnp.float32)
    inverse = jax.scipy.linalg.solve_triangular(upper_fac.T, identity, lower=True)
    return jnp.dot(matrix, inverse.T, precision=HIGHEST, preferred_element_type=jnp.float32)


def from_gram(gram_mat, matrix):
    upper_fac = jnp.linalg.cholesky(gram_mat).T
    return (upper_fac, from_upper(upper_fac, matrix))


def apply_operator(vector, diagonal, blocks, span_offsets, col_offsets):
    block_count = blocks.shape[0]
    block_size = blocks.shape[2]
    vec_width = vector.shape[1]
    lowered = vector.astype(jnp.bfloat16).reshape(1, block_count, block_size * vec_width)
    face_cells = padded(lowered, (("span", 0),), 1)
    extended = padded(face_cells, (("band", 1),), W)
    stride = block_count + 2 * W
    lookup = extended.reshape(3 * stride, block_size, vec_width)
    row_ids = jnp.arange(block_count, dtype=jnp.int32)[:, None]
    flat_index = (span_offsets + 1) * stride + row_ids + W + col_offsets
    picked = jnp.take(lookup, flat_index, axis=0)
    coupled = jnp.einsum("ikab,ikbc->iac", blocks, picked, preferred_element_type=jnp.float32)
    return diagonal[:, None] * vector + coupled.reshape(block_count * block_size, vec_width)


def subtract_projections(mapped, bases, coeffs):
    residual = mapped
    for position in range(len(bases)):
        residual = residual - jnp.dot(
            bases[position],
            coeffs[position],
            precision=HIGHEST,
            preferred_element_type=jnp.float32,
        )
    return residual


def plain_form(start_block, diagonal, blocks, span_offsets, col_offsets):
    row_total = float(start_block.shape[0] * lax.axis_size("span") * lax.axis_size("band"))
    vec_width = start_block.shape[1]
    first_gram = lax.psum(local_inner(start_block, start_block, row_total), ("span", "band"))
    r_first, current = from_gram(first_gram, start_block)
    bases = [current]
    columns = []
    for step_id in range(STEPS):
        mapped = apply_operator(bases[-1], diagonal, blocks, span_offsets, col_offsets)
        partials = jnp.stack([local_inner(earlier, mapped, row_total) for earlier in bases])
        coeffs = lax.psum(partials, ("span", "band"))
        residual = subtract_projections(mapped, bases, coeffs)
        gram_mat = lax.psum(local_inner(residual, residual, row_total), ("span", "band"))
        r_next, q_next = from_gram(gram_mat, residual)
        pieces = [coeffs.reshape(len(bases) * vec_width, vec_width), r_next]
        if STEPS - 1 - step_id > 0:
            pieces.append(jnp.zeros(((STEPS - 1 - step_id) * vec_width, vec_width), jnp.float32))
        columns.append(jnp.concatenate(pieces, axis=0))
        bases.append(q_next)
    hessenberg = jnp.concatenate(columns, axis=1)
    bases_out = jnp.stack(bases[1:])
    return (bases_out, hessenberg, r_first)


def dot(a, b):
    return jnp.dot(a, b, preferred_element_type=F32)


def dot_rows(a, b, precision=None):
    return lax.dot_general(
        a, b, (((0,), (0,)), ((), ())), precision=precision, preferred_element_type=F32
    )


def split2(x):
    high = x.astype(BF16)
    return high, (x - high.astype(F32)).astype(BF16)


def both(x):
    return jnp.concatenate(split2(x), axis=1)


def square(x):
    pair = both(x)
    return jnp.concatenate([pair, pair], axis=0)


def halves(x):
    n = x.shape[1] // 2
    return x[:, :n] + x[:, n:]


def quarters(x):
    n = x.shape[0] // 2
    return halves(x[:n] + x[n:])


def kernel(
    dims,
    start_ref,
    diag_ref,
    blocks_ref,
    spans_ref,
    cols_ref,
    bases_ref,
    hess_ref,
    first_ref,
    flag_ref,
    blk,
    ext,
    qf,
    qs,
    mf,
    dg,
    gram,
    work,
    fac,
    inv,
    hb,
    lb,
    part,
    recv1,
    mid,
    recv2,
    fin,
    total,
    cond,
    send_sem,
    recv_sem,
    halo_send,
    halo_recv,
    blk_sem,
    out_sem,
):
    n_span, n_band, nb, bs, width, kc = dims
    n_xy, n_zc = n_span // 2, n_band * 2
    rows = nb * bs
    stride = nb + 2 * W
    chunk = width // n_xy
    scale = 1.0 / (rows * n_span * n_band)
    s = lax.axis_index("span")
    z = lax.axis_index("band")
    xy, core = s // 2, s % 2
    zc = z * 2 + core

    def xy_peer(d):
        peer = lax.rem(xy + d, n_xy)
        return peer, (peer * 2 + core, z)

    def zc_peer(d):
        peer = lax.rem(zc + d, n_zc)
        return peer, (xy * 2 + lax.rem(peer, 2), peer // 2)

    ways = [(ds, db) for db in (0, -1, 1) for ds in (-1, 0, 1) if (ds, db) != (0, 0)]

    def reaches(ds, db):
        return (s + ds >= 0) & (s + ds < n_span) & (z + db >= 0) & (z + db < n_band)

    def halo_copy(n):
        ds, db = ways[n]
        seg = (1 - ds) * stride
        if db == 0:
            source, target, count = W, W, nb
        elif db == 1:
            source, target, count = nb, 0, W
        else:
            source, target, count = W, nb + W, W
        return pltpu.make_async_remote_copy(
            src_ref=ext.at[pl.ds(stride + source, count)],
            dst_ref=ext.at[pl.ds(seg + target, count)],
            send_sem=halo_send.at[n],
            recv_sem=halo_recv.at[n],
            device_id=(s + ds, z + db),
            device_id_type=MESH,
        )

    load = pltpu.make_async_copy(blocks_ref, blk, blk_sem)
    load.start()
    ext[...] = jnp.zeros_like(ext)
    barrier = pltpu.get_barrier_semaphore()

    def greet(peer_of):
        def body(d, carry):
            pl.semaphore_signal(barrier, inc=1, device_id=peer_of(d)[1], device_id_type=MESH)
            return carry

        return body

    lax.fori_loop(1, n_xy, greet(xy_peer), 0)
    lax.fori_loop(1, n_zc, greet(zc_peer), 0)
    for ds, db in ways:

        @pl.when(reaches(ds, db))
        def _():
            pl.semaphore_signal(barrier, inc=1, device_id=(s + ds, z + db), device_id_type=MESH)

    def accumulate(lefts, right):
        for m, left in enumerate(lefts):
            gram[m] = gram[m] + dot_rows(left, right)

    def publish(t, nm):
        for m in range(nm):
            part[t, :, m] = (quarters(gram[m]) * scale).reshape(n_xy, chunk, width)

    def all_reduce(t, nm, meanwhile=None):
        take = pl.ds(0, nm)
        par = t % 2

        def first(d):
            peer, device = xy_peer(d)
            return pltpu.make_async_remote_copy(
                src_ref=part.at[t, peer, take],
                dst_ref=recv1.at[t, xy, take],
                send_sem=send_sem.at[0, peer],
                recv_sem=recv_sem.at[par, 0, xy],
                device_id=device,
                device_id_type=MESH,
            )

        def second(d):
            peer, device = zc_peer(d)
            return pltpu.make_async_remote_copy(
                src_ref=mid.at[t, take],
                dst_ref=recv2.at[t, zc, take],
                send_sem=send_sem.at[1, peer],
                recv_sem=recv_sem.at[par, 1, zc],
                device_id=device,
                device_id_type=MESH,
            )

        def third(d):
            peer, device = xy_peer(d)
            return pltpu.make_async_remote_copy(
                src_ref=fin.at[t, take],
                dst_ref=total.at[t, xy, take],
                send_sem=send_sem.at[2, peer],
                recv_sem=recv_sem.at[par, 2, xy],
                device_id=device,
                device_id_type=MESH,
            )

        def landed(buffer, stage, who, like):
            peer, device = who
            pltpu.make_async_remote_copy(
                src_ref=like,
                dst_ref=buffer.at[t, peer, take],
                send_sem=send_sem.at[stage, peer],
                recv_sem=recv_sem.at[par, stage, peer],
                device_id=device,
                device_id_type=MESH,
            ).wait_recv()

        def each(n, act):
            def body(d, carry):
                act(d)
                return carry

            lax.fori_loop(1, n, body, 0)

        each(n_xy, lambda d: first(d).start())
        recv1[t, xy, :nm] = part[t, xy, :nm]
        if meanwhile is not None:
            meanwhile()
        each(n_xy, lambda d: landed(recv1, 0, xy_peer(d), mid.at[t, take]))
        value = recv1[t, 0, :nm]
        for i in range(1, n_xy):
            value = value + recv1[t, i, :nm]
        mid[t, :nm] = value
        each(n_zc, lambda d: second(d).start())
        recv2[t, zc, :nm] = value
        each(n_zc, lambda d: landed(recv2, 1, zc_peer(d), mid.at[t, take]))
        value = recv2[t, 0, :nm]
        for i in range(1, n_zc):
            value = value + recv2[t, i, :nm]
        fin[t, :nm] = value
        each(n_xy, lambda d: third(d).start())
        total[t, xy, :nm] = value
        each(n_xy, lambda d: landed(total, 2, xy_peer(d), fin.at[t, take]))
        each(n_xy, lambda d: first(d).wait_send())
        each(n_zc, lambda d: second(d).wait_send())
        each(n_xy, lambda d: third(d).wait_send())
        return [total[t, :, m].reshape(width, width) for m in range(nm)]

    def factor(matrix, beside):
        work[:, :width] = matrix
        eye = lax.broadcasted_iota(jnp.int32, (width, width), 0) == lax.broadcasted_iota(
            jnp.int32, (width, width), 1
        )
        work[:, width:] = jnp.where(eye, 1.0, 0.0).astype(F32)
        row = lax.broadcasted_iota(jnp.int32, (8, width), 0)
        lane = lax.broadcasted_iota(jnp.int32, (8, width), 1)

        def panel(p, carry):
            k0 = pl.multiple_of(p * 8, 8)
            own = pltpu.roll(work[pl.ds(k0, 8), :width], lax.rem(width - k0, width), 1)
            right = work[pl.ds(k0, 8), width:]
            beside(p)
            for j in range(8):
                column = jnp.broadcast_to(own[:, j : j + 1], (8, width))
                scaled = lax.rsqrt(jnp.broadcast_to(column[j : j + 1], (8, width)))
                column = column * scaled
                line = jnp.broadcast_to(own[j : j + 1], (8, width)) * scaled
                own = jnp.where(row > j, own - column * line, jnp.where(row == j, line, own))
                line = jnp.broadcast_to(right[j : j + 1], (8, width)) * scaled
                right = jnp.where(row > j, right - column * line, jnp.where(row == j, line, right))
            upper = jnp.where(lane >= k0 + row, pltpu.roll(own, k0, 1), 0.0)
            fac[pl.ds(k0, 8), :] = upper
            inv[pl.ds(k0, 8), :] = right
            both_parts = jnp.concatenate([upper, right], axis=1)
            later = jnp.where(lane >= k0 + 8, upper, 0.0)
            b1 = both_parts.astype(BF16).astype(F32)
            b2 = (both_parts - b1).astype(BF16).astype(F32)
            b3 = both_parts - b1 - b2
            a1 = later.astype(BF16).astype(F32)
            a2 = (later - a1).astype(BF16).astype(F32)
            a3 = later - a1 - a2
            left = jnp.concatenate([a1, a1, a2, a2, a1, a3], axis=0).astype(BF16)
            rights = jnp.concatenate([b1, b2, b1, b2, b3, b1], axis=0).astype(BF16)
            work[...] = work[...] - dot_rows(left, rights)
            return carry

        lax.fori_loop(0, width // 8, panel, 0)
        diag = jnp.sum(jnp.where(eye, carry_gram[0], 0.0), axis=0, keepdims=True)
        inverse = inv[...]
        cond[...] = cond[...] + diag * jnp.sum(inverse * inverse, axis=0, keepdims=True)
        lb[...] = square(inverse.T)

    carry_gram = [None]

    def form_basis(t):
        def body(i, carry):
            here = pl.ds(pl.multiple_of(i * bs, bs), bs)
            q = halves(dot(both(mf[here, :]), lb[...]))
            qf[t, here, :] = q
            if t < STEPS:
                high, low = split2(q)
                qs[t, here, :] = jnp.concatenate([high, low], axis=1)
                ext[stride + W + i] = high
            return carry

        lax.fori_loop(0, nb, body, 0)

    cond[...] = jnp.zeros_like(cond)
    hess_ref[...] = jnp.zeros_like(hess_ref)
    gram[0] = jnp.zeros_like(gram[0])

    def start_part(i, carry):
        here = pl.ds(pl.multiple_of(i * bs, bs), bs)
        value = start_ref[here, :]
        mf[here, :] = value
        pair = both(value)
        accumulate([pair], pair)
        return carry

    lax.fori_loop(0, nb, start_part, 0)
    publish(0, 1)
    beside_span = 3 - (s == 0).astype(jnp.int32) - (s == n_span - 1).astype(jnp.int32)
    beside_band = 3 - (z == 0).astype(jnp.int32) - (z == n_band - 1).astype(jnp.int32)
    pl.semaphore_wait(barrier, n_xy + n_zc - 3 + beside_span * beside_band)

    def expand_diag():
        def body(c, carry):
            line = jnp.broadcast_to(diag_ref[pl.ds(c, 1), :], (width, width))
            dg[pl.ds(pl.multiple_of(c * width, width), width), :] = line.T
            return carry

        lax.fori_loop(0, rows // width, body, 0)

    (matrix,) = all_reduce(0, 1, expand_diag)
    carry_gram[0] = matrix
    factor(matrix, lambda p: None)
    first_ref[...] = fac[...]
    form_basis(0)
    load.wait()

    for j in range(STEPS):
        for n, (ds, db) in enumerate(ways):

            @pl.when(reaches(ds, db))
            def _(n=n):
                halo_copy(n).start()

        for m in range(j + 2):
            gram[m] = jnp.zeros_like(gram[m])
        for n, (ds, db) in enumerate(ways):

            @pl.when(reaches(-ds, -db))
            def _(n=n):
                halo_copy(n).wait_recv()

        def block_row(i, carry, j=j):
            here = pl.ds(pl.multiple_of(i * bs, bs), bs)
            acc = dg[here, :] * qf[j, here, :]
            for k in range(kc):
                at = (spans_ref[i, k] + 1) * stride + i + W + cols_ref[i, k]
                acc = acc + dot(blk[i, k], ext[at])
            mf[here, :] = acc
            pair = both(acc)
            accumulate([qs[m, here, :] for m in range(j + 1)] + [pair], pair)
            return carry

        lax.fori_loop(0, nb, block_row, 0)
        publish(j + 1, j + 2)
        for n, (ds, db) in enumerate(ways):

            @pl.when(reaches(ds, db))
            def _(n=n):
                halo_copy(n).wait_send()

        sums = all_reduce(j + 1, j + 2)
        matrix = sums[j + 1]
        carry_gram[0] = matrix
        for i in range(j + 1):
            hess_ref[i * width : (i + 1) * width, j * width : (j + 1) * width] = sums[i]
            hb[i] = square(sums[i])
            matrix = matrix - dot_rows(sums[i], sums[i], HIGHEST)

        def residual_part(p, j=j):
            here = pl.ds(pl.multiple_of(p * (rows // (width // 8)), rows // (width // 8)), rows // (width // 8))
            value = mf[here, :]
            for i in range(j + 1):
                value = value - halves(dot(qs[i, here, :], hb[i]))
            mf[here, :] = value

        factor(matrix, residual_part)
        hess_ref[(j + 1) * width : (j + 2) * width, j * width : (j + 1) * width] = fac[...]
        form_basis(j + 1)
        pltpu.make_async_copy(qf.at[j + 1], bases_ref.at[j], out_sem.at[j]).start()

    flag_ref[0, 0] = jnp.sum(cond[...])
    for j in range(STEPS):
        pltpu.make_async_copy(qf.at[j + 1], bases_ref.at[j], out_sem.at[j]).wait()


def short_form(start_block, diagonal, blocks, span_offsets, col_offsets):
    n_span, n_band = lax.axis_size("span"), lax.axis_size("band")
    nb, kc, bs, _ = blocks.shape
    rows, width = start_block.shape
    dims = (n_span, n_band, nb, bs, width, kc)
    n_xy, n_zc = n_span // 2, n_band * 2
    stride = nb + 2 * W
    nm = STEPS + 1
    chunk = width // n_xy
    vmem = pl.BlockSpec(memory_space=pltpu.VMEM)
    smem = pl.BlockSpec(memory_space=pltpu.SMEM)
    anywhere = pl.BlockSpec(memory_space=pl.ANY)

    def body(*refs):
        kernel(dims, *refs)

    return pl.pallas_call(
        body,
        out_shape=(
            jax.ShapeDtypeStruct((STEPS, rows, width), F32),
            jax.ShapeDtypeStruct(((STEPS + 1) * width, STEPS * width), F32),
            jax.ShapeDtypeStruct((width, width), F32),
            jax.ShapeDtypeStruct((1, 1), F32),
        ),
        in_specs=[vmem, vmem, anywhere, smem, smem],
        out_specs=(anywhere, vmem, vmem, smem),
        scratch_shapes=[
            pltpu.VMEM((nb, kc, bs, bs), BF16),
            pltpu.VMEM((3 * stride, bs, width), BF16),
            pltpu.VMEM((STEPS + 1, rows, width), F32),
            pltpu.VMEM((STEPS, rows, 2 * width), BF16),
            pltpu.VMEM((rows, width), F32),
            pltpu.VMEM((rows, width), F32),
            pltpu.VMEM((nm, 2 * width, 2 * width), F32),
            pltpu.VMEM((width, 2 * width), F32),
            pltpu.VMEM((width, width), F32),
            pltpu.VMEM((width, width), F32),
            pltpu.VMEM((STEPS, 2 * width, 2 * width), BF16),
            pltpu.VMEM((2 * width, 2 * width), BF16),
            pltpu.VMEM((nm, n_xy, nm, chunk, width), F32),
            pltpu.VMEM((nm, n_xy, nm, chunk, width), F32),
            pltpu.VMEM((nm, nm, chunk, width), F32),
            pltpu.VMEM((nm, n_zc, nm, chunk, width), F32),
            pltpu.VMEM((nm, nm, chunk, width), F32),
            pltpu.VMEM((nm, n_xy, nm, chunk, width), F32),
            pltpu.VMEM((1, width), F32),
            pltpu.SemaphoreType.DMA((3, max(n_xy, n_zc))),
            pltpu.SemaphoreType.DMA((2, 3, max(n_xy, n_zc))),
            pltpu.SemaphoreType.DMA((8,)),
            pltpu.SemaphoreType.DMA((8,)),
            pltpu.SemaphoreType.DMA,
            pltpu.SemaphoreType.DMA((STEPS,)),
        ],
        compiler_params=pltpu.CompilerParams(
            collective_id=0, has_side_effects=True, vmem_limit_bytes=48 * 1024 * 1024
        ),
    )(start_block, diagonal.reshape(rows // width, width), blocks, span_offsets, col_offsets)


def per_device(start_block, diagonal, blocks, span_offsets, col_offsets):
    args = (start_block, diagonal, blocks, span_offsets, col_offsets)
    bases_out, hessenberg, r_first, spread = short_form(*args)
    return lax.cond(
        spread[0, 0] <= LIMIT,
        lambda: (bases_out, hessenberg, r_first),
        lambda: plain_form(*args),
    )


def solution(mesh):
    placed = (
        P(("span", "band"), None),
        P(("span", "band")),
        P(("span", "band"), None, None, None),
        P(("span", "band"), None),
        P(("span", "band"), None),
    )
    return jax.shard_map(
        per_device,
        mesh=mesh,
        in_specs=placed,
        out_specs=(P(None, ("span", "band"), None), P(), P()),
        check_vma=False,
    )
```

```python
import math

import jax
import jax.numpy as jnp
from jax import lax
from jax.experimental import pallas as pl
from jax.experimental.pallas import tpu as pltpu
from jax.sharding import PartitionSpec as P

W = 2
STEPS = 3
LIMIT = 16384.0
F32 = jnp.float32
BF16 = jnp.bfloat16
MESH = pl.DeviceIdType.MESH
HIGHEST = lax.Precision.HIGHEST


def padded(block, sides, width):
    for axis, dim in sides:
        count = lax.axis_size(axis)
        forward = [(i, i + 1) for i in range(count - 1)]
        backward = [(target, source) for source, target in forward]
        low = lax.ppermute(
            lax.slice_in_dim(block, block.shape[dim] - width, None, axis=dim), axis, forward
        )
        high = lax.ppermute(lax.slice_in_dim(block, 0, width, axis=dim), axis, backward)
        block = jnp.concatenate([low, block, high], axis=dim)
    return block


def local_inner(first, second, row_total):
    return (
        jnp.dot(first.T, second, precision=HIGHEST, preferred_element_type=jnp.float32) / row_total
    )


def sum_all(value):
    for axis in ("band", "span"):
        count = lax.axis_size(axis)
        bit = 1
        while bit < count:
            value = value + lax.ppermute(value, axis, [(i, i ^ bit) for i in range(count)])
            bit *= 2
    return value


def from_upper(upper_fac, matrix):
    identity = jnp.eye(upper_fac.shape[0], dtype=jnp.float32)
    inverse = jax.scipy.linalg.solve_triangular(upper_fac.T, identity, lower=True)
    return jnp.dot(matrix, inverse.T, precision=HIGHEST, preferred_element_type=jnp.float32)


def from_gram(gram_mat, matrix):
    upper_fac = jnp.linalg.cholesky(gram_mat).T
    return (upper_fac, from_upper(upper_fac, matrix))


def apply_operator(vector, diagonal, blocks, span_offsets, col_offsets):
    block_count = blocks.shape[0]
    block_size = blocks.shape[2]
    vec_width = vector.shape[1]
    lowered = vector.astype(jnp.bfloat16).reshape(1, block_count, block_size * vec_width)
    face_cells = padded(lowered, (("span", 0),), 1)
    extended = padded(face_cells, (("band", 1),), W)
    stride = block_count + 2 * W
    lookup = extended.reshape(3 * stride, block_size, vec_width)
    row_ids = jnp.arange(block_count, dtype=jnp.int32)[:, None]
    flat_index = (span_offsets + 1) * stride + row_ids + W + col_offsets
    picked = jnp.take(lookup, flat_index, axis=0)
    coupled = jnp.einsum("ikab,ikbc->iac", blocks, picked, preferred_element_type=jnp.float32)
    return diagonal[:, None] * vector + coupled.reshape(block_count * block_size, vec_width)


def subtract_projections(mapped, bases, coeffs):
    residual = mapped
    for position in range(len(bases)):
        residual = residual - jnp.dot(
            bases[position],
            coeffs[position],
            precision=HIGHEST,
            preferred_element_type=jnp.float32,
        )
    return residual


def plain_form(start_block, diagonal, blocks, span_offsets, col_offsets):
    row_total = float(start_block.shape[0] * lax.axis_size("span") * lax.axis_size("band"))
    vec_width = start_block.shape[1]
    first_gram = sum_all(local_inner(start_block, start_block, row_total))
    r_first, current = from_gram(first_gram, start_block)
    bases = [current]
    columns = []
    for step_id in range(STEPS):
        mapped = apply_operator(bases[-1], diagonal, blocks, span_offsets, col_offsets)
        partials = jnp.stack([local_inner(earlier, mapped, row_total) for earlier in bases])
        coeffs = sum_all(partials)
        residual = subtract_projections(mapped, bases, coeffs)
        gram_mat = sum_all(local_inner(residual, residual, row_total))
        r_next, q_next = from_gram(gram_mat, residual)
        pieces = [coeffs.reshape(len(bases) * vec_width, vec_width), r_next]
        if STEPS - 1 - step_id > 0:
            pieces.append(jnp.zeros(((STEPS - 1 - step_id) * vec_width, vec_width), jnp.float32))
        columns.append(jnp.concatenate(pieces, axis=0))
        bases.append(q_next)
    hessenberg = jnp.concatenate(columns, axis=1)
    bases_out = jnp.stack(bases[1:])
    return (bases_out, hessenberg, r_first)


def dot(a, b):
    return jnp.dot(a, b, preferred_element_type=F32)


def dot_rows(a, b, precision=None):
    return lax.dot_general(
        a, b, (((0,), (0,)), ((), ())), precision=precision, preferred_element_type=F32
    )


def rounded(x):
    return x.astype(BF16).astype(F32)


def split2(x):
    high = x.astype(BF16)
    return high, (x - high.astype(F32)).astype(BF16)


def both(x):
    return jnp.concatenate(split2(x), axis=1)


def square(x):
    pair = both(x)
    return jnp.concatenate([pair, pair], axis=0)


def halves(x):
    n = x.shape[1] // 2
    return x[:, :n] + x[:, n:]


def quarters(x):
    n = x.shape[0] // 2
    return halves(x[:n] + x[n:])


def kernel(
    dims,
    start_ref,
    diag_ref,
    blocks_ref,
    spans_ref,
    cols_ref,
    bases_ref,
    hess_ref,
    first_ref,
    flag_ref,
    blk,
    ext,
    qf,
    qs,
    mf,
    dg,
    gram,
    work,
    fac,
    inv,
    spread,
    hb,
    lb,
    part,
    recv1,
    mid,
    recv2,
    fin,
    total,
    cond,
    send_sem,
    recv_sem,
    halo_send,
    halo_recv,
    blk_sem,
    out_sem,
):
    n_span, n_band, nb, bs, width, kc = dims
    n_xy, n_zc = n_span // 2, n_band * 2
    rows = nb * bs
    stride = nb + 2 * W
    chunk = width // n_xy
    scale = 1.0 / (rows * n_span * n_band)
    s = lax.axis_index("span")
    z = lax.axis_index("band")
    xy, core = s // 2, s % 2
    zc = z * 2 + core

    def xy_peer(d):
        peer = lax.rem(xy + d, n_xy)
        return peer, (peer * 2 + core, z)

    def zc_peer(d):
        peer = lax.rem(zc + d, n_zc)
        return peer, (xy * 2 + lax.rem(peer, 2), peer // 2)

    side = math.isqrt(n_xy)
    x, y = xy // side, xy % side

    def hops(step, count):
        return min(step, count - step)

    def xy_far(act):
        steps = [(dx, dy) for dx in range(side) for dy in range(side) if dx or dy]
        for dx, dy in sorted(steps, key=lambda t: -hops(t[0], side) - hops(t[1], side)):
            peer = lax.rem(x + dx, side) * side + lax.rem(y + dy, side)
            act((peer, (peer * 2 + core, z)))

    def zc_far(act):
        steps = [(dz, dc) for dz in range(n_band) for dc in range(2) if dz or dc]
        for dz, dc in sorted(steps, key=lambda t: -2 * hops(t[0], n_band) - t[1]):
            to_z, to_core = lax.rem(z + dz, n_band), lax.rem(core + dc, 2)
            act((to_z * 2 + to_core, (xy * 2 + to_core, to_z)))

    ways = [(ds, db) for db in (0, -1, 1) for ds in (-1, 0, 1) if (ds, db) != (0, 0)]

    def reaches(ds, db):
        return (s + ds >= 0) & (s + ds < n_span) & (z + db >= 0) & (z + db < n_band)

    def halo_copy(n):
        ds, db = ways[n]
        seg = (1 - ds) * stride
        if db == 0:
            source, target, count = W, W, nb
        elif db == 1:
            source, target, count = nb, 0, W
        else:
            source, target, count = W, nb + W, W
        return pltpu.make_async_remote_copy(
            src_ref=ext.at[pl.ds(stride + source, count)],
            dst_ref=ext.at[pl.ds(seg + target, count)],
            send_sem=halo_send.at[n],
            recv_sem=halo_recv.at[n],
            device_id=(s + ds, z + db),
            device_id_type=MESH,
        )

    load = pltpu.make_async_copy(blocks_ref, blk, blk_sem)
    load.start()
    ext[...] = jnp.zeros_like(ext)
    barrier = pltpu.get_barrier_semaphore()

    def greet(peer_of):
        def body(d, carry):
            pl.semaphore_signal(barrier, inc=1, device_id=peer_of(d)[1], device_id_type=MESH)
            return carry

        return body

    lax.fori_loop(1, n_xy, greet(xy_peer), 0)
    lax.fori_loop(1, n_zc, greet(zc_peer), 0)
    for ds, db in ways:

        @pl.when(reaches(ds, db))
        def _():
            pl.semaphore_signal(barrier, inc=1, device_id=(s + ds, z + db), device_id_type=MESH)

    def accumulate(lefts, right):
        for m, left in enumerate(lefts):
            gram[m] = gram[m] + dot_rows(left, right)

    def publish(t, nm):
        for m in range(nm):
            part[t, :, m] = (quarters(gram[m]) * scale).reshape(n_xy, chunk, width)

    def all_reduce(t, nm, meanwhile=None):
        take = pl.ds(0, nm)
        par = t % 2

        def first(who):
            peer, device = who
            return pltpu.make_async_remote_copy(
                src_ref=part.at[t, peer, take],
                dst_ref=recv1.at[t, xy, take],
                send_sem=send_sem.at[0, peer],
                recv_sem=recv_sem.at[par, 0, xy],
                device_id=device,
                device_id_type=MESH,
            )

        def second(who):
            peer, device = who
            return pltpu.make_async_remote_copy(
                src_ref=mid.at[t, take],
                dst_ref=recv2.at[t, zc, take],
                send_sem=send_sem.at[1, peer],
                recv_sem=recv_sem.at[par, 1, zc],
                device_id=device,
                device_id_type=MESH,
            )

        def third(who):
            peer, device = who
            return pltpu.make_async_remote_copy(
                src_ref=fin.at[t, take],
                dst_ref=total.at[t, xy, take],
                send_sem=send_sem.at[2, peer],
                recv_sem=recv_sem.at[par, 2, xy],
                device_id=device,
                device_id_type=MESH,
            )

        def landed(buffer, stage, who, like):
            peer, device = who
            pltpu.make_async_remote_copy(
                src_ref=like,
                dst_ref=buffer.at[t, peer, take],
                send_sem=send_sem.at[stage, peer],
                recv_sem=recv_sem.at[par, stage, peer],
                device_id=device,
                device_id_type=MESH,
            ).wait_recv()

        def each(n, act):
            def body(d, carry):
                act(d)
                return carry

            lax.fori_loop(1, n, body, 0)

        xy_far(lambda who: first(who).start())
        recv1[t, xy, :nm] = part[t, xy, :nm]
        if meanwhile is not None:
            meanwhile()
        each(n_xy, lambda d: landed(recv1, 0, xy_peer(d), mid.at[t, take]))
        value = recv1[t, 0, :nm]
        for i in range(1, n_xy):
            value = value + recv1[t, i, :nm]
        mid[t, :nm] = value
        zc_far(lambda who: second(who).start())
        recv2[t, zc, :nm] = value
        each(n_zc, lambda d: landed(recv2, 1, zc_peer(d), mid.at[t, take]))
        value = recv2[t, 0, :nm]
        for i in range(1, n_zc):
            value = value + recv2[t, i, :nm]
        fin[t, :nm] = value
        xy_far(lambda who: third(who).start())
        total[t, xy, :nm] = value
        each(n_xy, lambda d: landed(total, 2, xy_peer(d), fin.at[t, take]))

        def sent():
            each(n_xy, lambda d: first(xy_peer(d)).wait_send())
            each(n_zc, lambda d: second(zc_peer(d)).wait_send())
            each(n_xy, lambda d: third(xy_peer(d)).wait_send())

        return [total[t, :, m].reshape(width, width) for m in range(nm)], sent

    def factor(matrix, beside):
        w = width
        tile = (8, w)
        work[:, :w] = matrix
        eye = lax.broadcasted_iota(jnp.int32, (w, w), 0) == lax.broadcasted_iota(
            jnp.int32, (w, w), 1
        )
        work[:, w:] = jnp.where(eye, 1.0, 0.0).astype(F32)
        row = lax.broadcasted_iota(jnp.int32, tile, 0)
        lane = lax.broadcasted_iota(jnp.int32, tile, 1)
        lanes = lax.broadcasted_iota(jnp.int32, (w, w), 1)
        within, group = lax.rem(lanes, 8), lanes // 8
        firsts = (group == 0) | (group == 1) | (group == 4)
        seconds = (group == 2) | (group == 3)
        thirds = group == 5

        def assemble(lines):
            out = lines[7]
            for j in range(6, -1, -1):
                out = jnp.where(row == j, lines[j], out)
            return out

        def panel(p, carry):
            k0 = pl.multiple_of(p * 8, 8)
            pivot = work[pl.ds(k0, 8), :w]
            for j in range(8):
                spread[j] = jnp.take_along_axis(pivot, jnp.broadcast_to(k0 + j, tile), axis=1)
            spread[8] = pivot
            spread[9] = work[pl.ds(k0, 8), w:]
            columns = jnp.take_along_axis(work[:, :w], k0 + within, axis=1)
            a1 = rounded(columns)
            a2 = rounded(columns - a1)
            a3 = columns - a1 - a2
            left = jnp.where(firsts, a1, jnp.where(seconds, a2, jnp.where(thirds, a3, 0.0)))
            left = left.astype(BF16)[:, :48]

            def line(n, i):
                return jnp.broadcast_to(spread[n, pl.ds(i, 1), :], tile)

            a = [[line(j, i) if i >= j else None for j in range(8)] for i in range(8)]
            heads = [line(8, i) for i in range(8)]
            tails = [line(9, i) for i in range(8)]
            beside(p)
            by = [None] * 8
            for j in range(8):
                by[j] = lax.rsqrt(a[j][j])
                heads[j] = heads[j] * by[j]
                tails[j] = tails[j] * by[j]
                for i in range(j + 1, 8):
                    a[i][j] = a[i][j] * by[j]
                for i in range(j + 1, 8):
                    for m in range(j + 1, i + 1):
                        a[i][m] = a[i][m] - a[i][j] * a[m][j]
                    heads[i] = heads[i] - a[i][j] * heads[j]
                    tails[i] = tails[i] - a[i][j] * tails[j]
            fac[pl.ds(k0, 8), :] = jnp.where(lane >= k0 + row, assemble(heads), 0.0)
            inv[pl.ds(k0, 8), :] = assemble(tails)
            for j in range(7, -1, -1):
                heads[j] = heads[j] * by[j]
                tails[j] = tails[j] * by[j]
                for i in range(j):
                    heads[i] = heads[i] - a[j][i] * heads[j]
                    tails[i] = tails[i] - a[j][i] * tails[j]
            right = jnp.concatenate([assemble(heads), assemble(tails)], axis=1)
            b1 = rounded(right)
            b2 = rounded(right - b1)
            b3 = right - b1 - b2
            rights = jnp.concatenate([b1, b2, b1, b2, b3, b1], axis=0).astype(BF16)
            work[...] = work[...] - dot(left, rights)
            return carry

        lax.fori_loop(0, w // 8, panel, 0)
        inverse = inv[...]
        lb[...] = square(inverse.T)
        diag = jnp.sum(jnp.where(eye, carry_gram[0], 0.0), axis=0, keepdims=True)
        cond[...] = cond[...] + diag * jnp.sum(inverse * inverse, axis=0, keepdims=True)

    carry_gram = [None]

    def form_basis(t):
        def body(i, carry):
            here = pl.ds(pl.multiple_of(i * bs, bs), bs)
            q = halves(dot(both(mf[here, :]), lb[...]))
            qf[t, here, :] = q
            if t < STEPS:
                high, low = split2(q)
                qs[t, here, :] = jnp.concatenate([high, low], axis=1)
                ext[stride + W + i] = high
            return carry

        lax.fori_loop(0, nb, body, 0)

    cond[...] = jnp.zeros_like(cond)
    hess_ref[...] = jnp.zeros_like(hess_ref)
    gram[0] = jnp.zeros_like(gram[0])

    def start_part(i, carry):
        here = pl.ds(pl.multiple_of(i * bs, bs), bs)
        value = start_ref[here, :]
        mf[here, :] = value
        pair = both(value)
        accumulate([pair], pair)
        return carry

    lax.fori_loop(0, nb, start_part, 0)
    publish(0, 1)
    beside_span = 3 - (s == 0).astype(jnp.int32) - (s == n_span - 1).astype(jnp.int32)
    beside_band = 3 - (z == 0).astype(jnp.int32) - (z == n_band - 1).astype(jnp.int32)
    pl.semaphore_wait(barrier, n_xy + n_zc - 3 + beside_span * beside_band)

    def expand_diag():
        def body(c, carry):
            line = jnp.broadcast_to(diag_ref[pl.ds(c, 1), :], (width, width))
            dg[pl.ds(pl.multiple_of(c * width, width), width), :] = line.T
            return carry

        lax.fori_loop(0, rows // width, body, 0)

    (matrix,), sent = all_reduce(0, 1, expand_diag)
    carry_gram[0] = matrix
    factor(matrix, lambda p: None)
    first_ref[...] = fac[...]
    form_basis(0)
    load.wait()

    for j in range(STEPS):
        for n, (ds, db) in enumerate(ways):

            @pl.when(reaches(ds, db))
            def _(n=n):
                halo_copy(n).start()

        sent()
        for m in range(j + 2):
            gram[m] = jnp.zeros_like(gram[m])
        for n, (ds, db) in enumerate(ways):

            @pl.when(reaches(-ds, -db))
            def _(n=n):
                halo_copy(n).wait_recv()

        def block_row(i, carry, j=j):
            here = pl.ds(pl.multiple_of(i * bs, bs), bs)
            acc = dg[here, :] * qf[j, here, :]
            for k in range(kc):
                at = (spans_ref[i, k] + 1) * stride + i + W + cols_ref[i, k]
                acc = acc + dot(blk[i, k], ext[at])
            mf[here, :] = acc
            pair = both(acc)
            accumulate([qs[m, here, :] for m in range(j + 1)] + [pair], pair)
            return carry

        lax.fori_loop(0, nb, block_row, 0)
        publish(j + 1, j + 2)
        def halo_sent():
            for n, (ds, db) in enumerate(ways):

                @pl.when(reaches(ds, db))
                def _(n=n):
                    halo_copy(n).wait_send()

        sums, sent = all_reduce(j + 1, j + 2, halo_sent)
        matrix = sums[j + 1]
        carry_gram[0] = matrix
        for i in range(j + 1):
            hess_ref[i * width : (i + 1) * width, j * width : (j + 1) * width] = sums[i]
            hb[i] = square(sums[i])
            matrix = matrix - dot_rows(sums[i], sums[i], HIGHEST)

        def residual_part(p, j=j):
            here = pl.ds(pl.multiple_of(p * (rows // (width // 8)), rows // (width // 8)), rows // (width // 8))
            value = mf[here, :]
            for i in range(j + 1):
                value = value - halves(dot(qs[i, here, :], hb[i]))
            mf[here, :] = value

        factor(matrix, residual_part)
        hess_ref[(j + 1) * width : (j + 2) * width, j * width : (j + 1) * width] = fac[...]
        form_basis(j + 1)
        pltpu.make_async_copy(qf.at[j + 1], bases_ref.at[j], out_sem.at[j]).start()

    sent()
    flag_ref[0, 0] = jnp.sum(cond[...])
    for j in range(STEPS):
        pltpu.make_async_copy(qf.at[j + 1], bases_ref.at[j], out_sem.at[j]).wait()


def short_form(start_block, diagonal, blocks, span_offsets, col_offsets):
    n_span, n_band = lax.axis_size("span"), lax.axis_size("band")
    nb, kc, bs, _ = blocks.shape
    rows, width = start_block.shape
    dims = (n_span, n_band, nb, bs, width, kc)
    n_xy, n_zc = n_span // 2, n_band * 2
    stride = nb + 2 * W
    nm = STEPS + 1
    chunk = width // n_xy
    vmem = pl.BlockSpec(memory_space=pltpu.VMEM)
    smem = pl.BlockSpec(memory_space=pltpu.SMEM)
    anywhere = pl.BlockSpec(memory_space=pl.ANY)

    def body(*refs):
        kernel(dims, *refs)

    return pl.pallas_call(
        body,
        out_shape=(
            jax.ShapeDtypeStruct((STEPS, rows, width), F32),
            jax.ShapeDtypeStruct(((STEPS + 1) * width, STEPS * width), F32),
            jax.ShapeDtypeStruct((width, width), F32),
            jax.ShapeDtypeStruct((1, 1), F32),
        ),
        in_specs=[vmem, vmem, anywhere, smem, smem],
        out_specs=(anywhere, vmem, vmem, smem),
        scratch_shapes=[
            pltpu.VMEM((nb, kc, bs, bs), BF16),
            pltpu.VMEM((3 * stride, bs, width), BF16),
            pltpu.VMEM((STEPS + 1, rows, width), F32),
            pltpu.VMEM((STEPS, rows, 2 * width), BF16),
            pltpu.VMEM((rows, width), F32),
            pltpu.VMEM((rows, width), F32),
            pltpu.VMEM((nm, 2 * width, 2 * width), F32),
            pltpu.VMEM((width, 2 * width), F32),
            pltpu.VMEM((width, width), F32),
            pltpu.VMEM((width, width), F32),
            pltpu.VMEM((10, 8, width), F32),
            pltpu.VMEM((STEPS, 2 * width, 2 * width), BF16),
            pltpu.VMEM((2 * width, 2 * width), BF16),
            pltpu.VMEM((nm, n_xy, nm, chunk, width), F32),
            pltpu.VMEM((nm, n_xy, nm, chunk, width), F32),
            pltpu.VMEM((nm, nm, chunk, width), F32),
            pltpu.VMEM((nm, n_zc, nm, chunk, width), F32),
            pltpu.VMEM((nm, nm, chunk, width), F32),
            pltpu.VMEM((nm, n_xy, nm, chunk, width), F32),
            pltpu.VMEM((1, width), F32),
            pltpu.SemaphoreType.DMA((3, max(n_xy, n_zc))),
            pltpu.SemaphoreType.DMA((2, 3, max(n_xy, n_zc))),
            pltpu.SemaphoreType.DMA((8,)),
            pltpu.SemaphoreType.DMA((8,)),
            pltpu.SemaphoreType.DMA,
            pltpu.SemaphoreType.DMA((STEPS,)),
        ],
        compiler_params=pltpu.CompilerParams(
            collective_id=0, has_side_effects=True, vmem_limit_bytes=48 * 1024 * 1024
        ),
    )(start_block, diagonal.reshape(rows // width, width), blocks, span_offsets, col_offsets)


def hand_over(bases_out, hessenberg, r_first):
    parts = bases_out.shape[0]

    def body(bases, hess, first, bases_to, hess_to, first_to, sems):
        copies = [
            pltpu.make_async_copy(bases.at[i], bases_to.at[i], sems.at[i]) for i in range(parts)
        ]
        copies.append(pltpu.make_async_copy(hess, hess_to, sems.at[parts]))
        copies.append(pltpu.make_async_copy(first, first_to, sems.at[parts + 1]))
        for copy in copies:
            copy.start()
        for copy in copies:
            copy.wait()

    arrays = (bases_out, hessenberg, r_first)
    anywhere = pl.BlockSpec(memory_space=pl.ANY)
    return pl.pallas_call(
        body,
        out_shape=tuple(jax.ShapeDtypeStruct(a.shape, a.dtype) for a in arrays),
        in_specs=[anywhere] * 3,
        out_specs=(anywhere,) * 3,
        scratch_shapes=[pltpu.SemaphoreType.DMA((parts + 2,))],
    )(*arrays)


def per_device(start_block, diagonal, blocks, span_offsets, col_offsets):
    args = (start_block, diagonal, blocks, span_offsets, col_offsets)
    bases_out, hessenberg, r_first, spread = short_form(*args)
    return lax.cond(
        spread[0, 0] <= LIMIT,
        lambda: hand_over(bases_out, hessenberg, r_first),
        lambda: plain_form(*args),
    )


def solution(mesh):
    placed = (
        P(("span", "band"), None),
        P(("span", "band")),
        P(("span", "band"), None, None, None),
        P(("span", "band"), None),
        P(("span", "band"), None),
    )
    return jax.shard_map(
        per_device,
        mesh=mesh,
        in_specs=placed,
        out_specs=(P(None, ("span", "band"), None), P(), P()),
        check_vma=False,
    )
```

```python
import math

import jax
import jax.numpy as jnp
from jax import lax
from jax.experimental import pallas as pl
from jax.experimental.pallas import tpu as pltpu
from jax.sharding import PartitionSpec as P

W = 2
STEPS = 3
LIMIT = 16384.0
F32 = jnp.float32
BF16 = jnp.bfloat16
MESH = pl.DeviceIdType.MESH
HIGHEST = lax.Precision.HIGHEST


def padded(block, sides, width):
    for axis, dim in sides:
        count = lax.axis_size(axis)
        forward = [(i, i + 1) for i in range(count - 1)]
        backward = [(target, source) for source, target in forward]
        low = lax.ppermute(
            lax.slice_in_dim(block, block.shape[dim] - width, None, axis=dim), axis, forward
        )
        high = lax.ppermute(lax.slice_in_dim(block, 0, width, axis=dim), axis, backward)
        block = jnp.concatenate([low, block, high], axis=dim)
    return block


def local_inner(first, second, row_total):
    return (
        jnp.dot(first.T, second, precision=HIGHEST, preferred_element_type=jnp.float32) / row_total
    )


def sum_all(value):
    for axis in ("band", "span"):
        count = lax.axis_size(axis)
        bit = 1
        while bit < count:
            value = value + lax.ppermute(value, axis, [(i, i ^ bit) for i in range(count)])
            bit *= 2
    return value


def from_upper(upper_fac, matrix):
    identity = jnp.eye(upper_fac.shape[0], dtype=jnp.float32)
    inverse = jax.scipy.linalg.solve_triangular(upper_fac.T, identity, lower=True)
    return jnp.dot(matrix, inverse.T, precision=HIGHEST, preferred_element_type=jnp.float32)


def from_gram(gram_mat, matrix):
    upper_fac = jnp.linalg.cholesky(gram_mat).T
    return (upper_fac, from_upper(upper_fac, matrix))


def apply_operator(vector, diagonal, blocks, span_offsets, col_offsets):
    block_count = blocks.shape[0]
    block_size = blocks.shape[2]
    vec_width = vector.shape[1]
    lowered = vector.astype(jnp.bfloat16).reshape(1, block_count, block_size * vec_width)
    face_cells = padded(lowered, (("span", 0),), 1)
    extended = padded(face_cells, (("band", 1),), W)
    stride = block_count + 2 * W
    lookup = extended.reshape(3 * stride, block_size, vec_width)
    row_ids = jnp.arange(block_count, dtype=jnp.int32)[:, None]
    flat_index = (span_offsets + 1) * stride + row_ids + W + col_offsets
    picked = jnp.take(lookup, flat_index, axis=0)
    coupled = jnp.einsum("ikab,ikbc->iac", blocks, picked, preferred_element_type=jnp.float32)
    return diagonal[:, None] * vector + coupled.reshape(block_count * block_size, vec_width)


def subtract_projections(mapped, bases, coeffs):
    residual = mapped
    for position in range(len(bases)):
        residual = residual - jnp.dot(
            bases[position],
            coeffs[position],
            precision=HIGHEST,
            preferred_element_type=jnp.float32,
        )
    return residual


def plain_form(start_block, diagonal, blocks, span_offsets, col_offsets):
    row_total = float(start_block.shape[0] * lax.axis_size("span") * lax.axis_size("band"))
    vec_width = start_block.shape[1]
    first_gram = sum_all(local_inner(start_block, start_block, row_total))
    r_first, current = from_gram(first_gram, start_block)
    bases = [current]
    columns = []
    for step_id in range(STEPS):
        mapped = apply_operator(bases[-1], diagonal, blocks, span_offsets, col_offsets)
        partials = jnp.stack([local_inner(earlier, mapped, row_total) for earlier in bases])
        coeffs = sum_all(partials)
        residual = subtract_projections(mapped, bases, coeffs)
        gram_mat = sum_all(local_inner(residual, residual, row_total))
        r_next, q_next = from_gram(gram_mat, residual)
        pieces = [coeffs.reshape(len(bases) * vec_width, vec_width), r_next]
        if STEPS - 1 - step_id > 0:
            pieces.append(jnp.zeros(((STEPS - 1 - step_id) * vec_width, vec_width), jnp.float32))
        columns.append(jnp.concatenate(pieces, axis=0))
        bases.append(q_next)
    hessenberg = jnp.concatenate(columns, axis=1)
    bases_out = jnp.stack(bases[1:])
    return (bases_out, hessenberg, r_first)


def dot(a, b):
    return jnp.dot(a, b, preferred_element_type=F32)


def dot_rows(a, b, precision=None):
    return lax.dot_general(
        a, b, (((0,), (0,)), ((), ())), precision=precision, preferred_element_type=F32
    )


def rounded(x):
    return x.astype(BF16).astype(F32)


def split2(x):
    high = x.astype(BF16)
    return high, (x - high.astype(F32)).astype(BF16)


def both(x):
    return jnp.concatenate(split2(x), axis=1)


def square(x):
    pair = both(x)
    return jnp.concatenate([pair, pair], axis=0)


def halves(x):
    n = x.shape[1] // 2
    return x[:, :n] + x[:, n:]


def quarters(x):
    n = x.shape[0] // 2
    return halves(x[:n] + x[n:])


def kernel(
    dims,
    start_ref,
    diag_ref,
    blocks_ref,
    spans_ref,
    cols_ref,
    bases_ref,
    rest_ref,
    inverse_ref,
    hess_ref,
    first_ref,
    flag_ref,
    blk,
    ext,
    qf,
    qs,
    mf,
    dg,
    gram,
    work,
    fac,
    inv,
    spread,
    hb,
    lb,
    part,
    recv1,
    mid,
    recv2,
    fin,
    total,
    cond,
    send_sem,
    recv_sem,
    halo_send,
    halo_recv,
    blk_sem,
    out_sem,
):
    n_span, n_band, nb, bs, width, kc = dims
    n_xy, n_zc = n_span // 2, n_band * 2
    rows = nb * bs
    stride = nb + 2 * W
    chunk = width // n_xy
    scale = 1.0 / (rows * n_span * n_band)
    s = lax.axis_index("span")
    z = lax.axis_index("band")
    xy, core = s // 2, s % 2
    zc = z * 2 + core

    def xy_peer(d):
        peer = lax.rem(xy + d, n_xy)
        return peer, (peer * 2 + core, z)

    def zc_peer(d):
        peer = lax.rem(zc + d, n_zc)
        return peer, (xy * 2 + lax.rem(peer, 2), peer // 2)

    side = math.isqrt(n_xy)
    x, y = xy // side, xy % side

    def hops(step, count):
        return min(step, count - step)

    def xy_far(act):
        steps = [(dx, dy) for dx in range(side) for dy in range(side) if dx or dy]
        for dx, dy in sorted(steps, key=lambda t: -hops(t[0], side) - hops(t[1], side)):
            peer = lax.rem(x + dx, side) * side + lax.rem(y + dy, side)
            act((peer, (peer * 2 + core, z)))

    def zc_far(act):
        steps = [(dz, dc) for dz in range(n_band) for dc in range(2) if dz or dc]
        for dz, dc in sorted(steps, key=lambda t: -2 * hops(t[0], n_band) - t[1]):
            to_z, to_core = lax.rem(z + dz, n_band), lax.rem(core + dc, 2)
            act((to_z * 2 + to_core, (xy * 2 + to_core, to_z)))

    sibling, beyond = s + 1 - 2 * core, s - 1 + 2 * core
    has_beyond = (beyond >= 0) & (beyond < n_span)
    has_below, has_above = z > 0, z < n_band - 1
    near_seg, far_seg = (2 - 2 * core) * stride, 2 * core * stride
    always = z >= 0
    low, high = W, nb
    top = nb + W

    moves = [
        (stride + low, near_seg + low, W, (beyond, z), has_beyond, far_seg + low, has_beyond),
        (stride + high, near_seg + high, W, (beyond, z), has_beyond, far_seg + high, has_beyond),
        (stride + low, stride + top, W, (s, z - 1), has_below, stride + top, has_above),
        (stride + high, stride, W, (s, z + 1), has_above, stride, has_below),
        (stride + low, far_seg + low, nb, (sibling, z), always, near_seg + low, always),
        (
            stride + low + W,
            near_seg + low + W,
            nb - 2 * W,
            (beyond, z),
            has_beyond,
            far_seg + low + W,
            has_beyond,
        ),
        (stride, far_seg, W, (sibling, z), has_below, near_seg, has_below),
        (stride + top, far_seg + top, W, (sibling, z), has_above, near_seg + top, has_above),
        (
            far_seg + high,
            far_seg,
            W,
            (s, z + 1),
            has_beyond & has_above,
            far_seg,
            has_beyond & has_below,
        ),
        (
            far_seg + low,
            far_seg + top,
            W,
            (s, z - 1),
            has_beyond & has_below,
            far_seg + top,
            has_beyond & has_above,
        ),
    ]

    def move(n, source, target, count, device):
        return pltpu.make_async_remote_copy(
            src_ref=ext.at[pl.ds(source, count)],
            dst_ref=ext.at[pl.ds(target, count)],
            send_sem=halo_send.at[n],
            recv_sem=halo_recv.at[n],
            device_id=device,
            device_id_type=MESH,
        )

    def send(*chosen):
        for n in chosen:
            source, target, count, device, goes, _, _ = moves[n]

            @pl.when(goes)
            def _():
                move(n, source, target, count, device).start()

    def sent_halo(*chosen):
        for n in chosen:
            source, target, count, device, goes, _, _ = moves[n]

            @pl.when(goes)
            def _():
                move(n, source, target, count, device).wait_send()

    def arrived(*chosen):
        for n in chosen:
            source, _, count, device, _, here, comes = moves[n]

            @pl.when(comes)
            def _():
                move(n, source, here, count, device).wait_recv()

    barrier = pltpu.get_barrier_semaphore()

    def greet(peer_of):
        def body(d, carry):
            pl.semaphore_signal(barrier, inc=1, device_id=peer_of(d)[1], device_id_type=MESH)
            return carry

        return body

    lax.fori_loop(1, n_xy, greet(xy_peer), 0)
    lax.fori_loop(1, n_zc, greet(zc_peer), 0)

    @pl.when(has_beyond)
    def _():
        pl.semaphore_signal(barrier, inc=1, device_id=(beyond, z), device_id_type=MESH)

    load = pltpu.make_async_copy(blocks_ref, blk, blk_sem)
    load.start()

    def accumulate(lefts, right):
        for m, left in enumerate(lefts):
            gram[m] = gram[m] + dot_rows(left, right)

    def publish(t, nm):
        for m in range(nm):
            part[t, :, m] = (quarters(gram[m]) * scale).reshape(n_xy, chunk, width)

    def all_reduce(t, nm, meanwhile=None):
        take = pl.ds(0, nm)
        par = t % 2

        def first(who):
            peer, device = who
            return pltpu.make_async_remote_copy(
                src_ref=part.at[t, peer, take],
                dst_ref=recv1.at[t, xy, take],
                send_sem=send_sem.at[0, peer],
                recv_sem=recv_sem.at[par, 0, xy],
                device_id=device,
                device_id_type=MESH,
            )

        def second(who):
            peer, device = who
            return pltpu.make_async_remote_copy(
                src_ref=mid.at[t, take],
                dst_ref=recv2.at[t, zc, take],
                send_sem=send_sem.at[1, peer],
                recv_sem=recv_sem.at[par, 1, zc],
                device_id=device,
                device_id_type=MESH,
            )

        def third(who):
            peer, device = who
            return pltpu.make_async_remote_copy(
                src_ref=fin.at[t, take],
                dst_ref=total.at[t, xy, take],
                send_sem=send_sem.at[2, peer],
                recv_sem=recv_sem.at[par, 2, xy],
                device_id=device,
                device_id_type=MESH,
            )

        def landed(buffer, stage, who, like):
            peer, device = who
            pltpu.make_async_remote_copy(
                src_ref=like,
                dst_ref=buffer.at[t, peer, take],
                send_sem=send_sem.at[stage, peer],
                recv_sem=recv_sem.at[par, stage, peer],
                device_id=device,
                device_id_type=MESH,
            ).wait_recv()

        def each(n, act):
            def body(d, carry):
                act(d)
                return carry

            lax.fori_loop(1, n, body, 0)

        xy_far(lambda who: first(who).start())
        recv1[t, xy, :nm] = part[t, xy, :nm]
        if meanwhile is not None:
            meanwhile()
        each(n_xy, lambda d: landed(recv1, 0, xy_peer(d), mid.at[t, take]))
        value = recv1[t, 0, :nm]
        for i in range(1, n_xy):
            value = value + recv1[t, i, :nm]
        mid[t, :nm] = value
        zc_far(lambda who: second(who).start())
        recv2[t, zc, :nm] = value
        each(n_zc, lambda d: landed(recv2, 1, zc_peer(d), mid.at[t, take]))
        value = recv2[t, 0, :nm]
        for i in range(1, n_zc):
            value = value + recv2[t, i, :nm]
        fin[t, :nm] = value
        xy_far(lambda who: third(who).start())
        total[t, xy, :nm] = value
        each(n_xy, lambda d: landed(total, 2, xy_peer(d), fin.at[t, take]))

        def sent():
            each(n_xy, lambda d: first(xy_peer(d)).wait_send())
            each(n_zc, lambda d: second(zc_peer(d)).wait_send())
            each(n_xy, lambda d: third(xy_peer(d)).wait_send())

        return [total[t, :, m].reshape(width, width) for m in range(nm)], sent

    def factor(matrix, beside):
        w = width
        tile = (8, w)
        work[:, :w] = matrix
        eye = lax.broadcasted_iota(jnp.int32, (w, w), 0) == lax.broadcasted_iota(
            jnp.int32, (w, w), 1
        )
        work[:, w:] = jnp.where(eye, 1.0, 0.0).astype(F32)
        row = lax.broadcasted_iota(jnp.int32, tile, 0)
        lane = lax.broadcasted_iota(jnp.int32, tile, 1)
        lanes = lax.broadcasted_iota(jnp.int32, (w, w), 1)
        within, group = lax.rem(lanes, 8), lanes // 8
        firsts = (group == 0) | (group == 1) | (group == 4)
        seconds = (group == 2) | (group == 3)
        thirds = group == 5

        def assemble(lines):
            out = lines[7]
            for j in range(6, -1, -1):
                out = jnp.where(row == j, lines[j], out)
            return out

        def panel(p, carry):
            k0 = pl.multiple_of(p * 8, 8)
            pivot = work[pl.ds(k0, 8), :w]
            for j in range(8):
                spread[j] = jnp.take_along_axis(pivot, jnp.broadcast_to(k0 + j, tile), axis=1)
            spread[8] = pivot
            spread[9] = work[pl.ds(k0, 8), w:]
            columns = jnp.take_along_axis(work[:, :w], k0 + within, axis=1)
            a1 = rounded(columns)
            a2 = rounded(columns - a1)
            a3 = columns - a1 - a2
            left = jnp.where(firsts, a1, jnp.where(seconds, a2, jnp.where(thirds, a3, 0.0)))
            left = left.astype(BF16)[:, :48]

            def line(n, i):
                return jnp.broadcast_to(spread[n, pl.ds(i, 1), :], tile)

            a = [[line(j, i) if i >= j else None for j in range(8)] for i in range(8)]
            heads = [line(8, i) for i in range(8)]
            tails = [line(9, i) for i in range(8)]
            beside(p)
            by = [None] * 8
            for j in range(8):
                by[j] = lax.rsqrt(a[j][j])
                heads[j] = heads[j] * by[j]
                tails[j] = tails[j] * by[j]
                for i in range(j + 1, 8):
                    a[i][j] = a[i][j] * by[j]
                for i in range(j + 1, 8):
                    for m in range(j + 1, i + 1):
                        a[i][m] = a[i][m] - a[i][j] * a[m][j]
                    heads[i] = heads[i] - a[i][j] * heads[j]
                    tails[i] = tails[i] - a[i][j] * tails[j]
            fac[pl.ds(k0, 8), :] = jnp.where(lane >= k0 + row, assemble(heads), 0.0)
            inv[pl.ds(k0, 8), :] = assemble(tails)
            for j in range(7, -1, -1):
                heads[j] = heads[j] * by[j]
                tails[j] = tails[j] * by[j]
                for i in range(j):
                    heads[i] = heads[i] - a[j][i] * heads[j]
                    tails[i] = tails[i] - a[j][i] * tails[j]
            right = jnp.concatenate([assemble(heads), assemble(tails)], axis=1)
            b1 = rounded(right)
            b2 = rounded(right - b1)
            b3 = right - b1 - b2
            rights = jnp.concatenate([b1, b2, b1, b2, b3, b1], axis=0).astype(BF16)
            work[...] = work[...] - dot(left, rights)
            return carry

        lax.fori_loop(0, w // 8, panel, 0)
        inverse = inv[...]
        lb[...] = square(inverse.T)
        diag = jnp.sum(jnp.where(eye, carry_gram[0], 0.0), axis=0, keepdims=True)
        cond[...] = cond[...] + diag * jnp.sum(inverse * inverse, axis=0, keepdims=True)

    carry_gram = [None]

    def form_basis(t):
        def form(i):
            here = pl.ds(pl.multiple_of(i * bs, bs), bs)
            q = halves(dot(both(mf[here, :]), lb[...]))
            qf[t, here, :] = q
            high, low = split2(q)
            qs[t, here, :] = jnp.concatenate([high, low], axis=1)
            ext[stride + W + i] = high

        def ends(e, carry):
            form(jnp.where(e < W, e, e + nb - 2 * W))
            return carry

        def middle(i, carry):
            form(i)
            return carry

        lax.fori_loop(0, 2 * W, ends, 0)
        send(0, 1, 2, 3)
        lax.fori_loop(W, nb - W, middle, 0)
        send(4, 5)

    cond[...] = jnp.zeros_like(cond)
    hess_ref[...] = jnp.zeros_like(hess_ref)
    gram[0] = jnp.zeros_like(gram[0])

    def start_part(i, carry):
        here = pl.ds(pl.multiple_of(i * bs, bs), bs)
        value = start_ref[here, :]
        mf[here, :] = value
        pair = both(value)
        accumulate([pair], pair)
        return carry

    lax.fori_loop(0, nb, start_part, 0)
    publish(0, 1)
    pl.semaphore_wait(barrier, n_xy + n_zc - 2 + has_beyond.astype(jnp.int32))

    def expand_diag():
        ext[...] = jnp.zeros_like(ext)

        def body(c, carry):
            line = jnp.broadcast_to(diag_ref[pl.ds(c, 1), :], (width, width))
            dg[pl.ds(pl.multiple_of(c * width, width), width), :] = line.T
            return carry

        lax.fori_loop(0, rows // width, body, 0)

    (matrix,), sent = all_reduce(0, 1, expand_diag)
    carry_gram[0] = matrix
    factor(matrix, lambda p: None)
    first_ref[...] = fac[...]
    load.wait()

    for j in range(STEPS):
        form_basis(j)
        if j > 0:
            pltpu.make_async_copy(qf.at[j], bases_ref.at[j - 1], out_sem.at[j - 1]).start()
        sent()
        for m in range(j + 2):
            gram[m] = jnp.zeros_like(gram[m])
        arrived(3)
        send(6)
        arrived(2)
        send(7)
        arrived(1)
        send(8)
        arrived(0)
        send(9)
        arrived(4, 5, 6, 7, 8, 9)

        def block_row(i, carry, j=j):
            here = pl.ds(pl.multiple_of(i * bs, bs), bs)
            acc = dg[here, :] * qf[j, here, :]
            for k in range(kc):
                at = (spans_ref[i, k] + 1) * stride + i + W + cols_ref[i, k]
                acc = acc + dot(blk[i, k], ext[at])
            mf[here, :] = acc
            pair = both(acc)
            accumulate([qs[m, here, :] for m in range(j + 1)] + [pair], pair)
            return carry

        lax.fori_loop(0, nb, block_row, 0)
        sent_halo(6, 7, 8, 9)
        publish(j + 1, j + 2)
        sums, sent = all_reduce(j + 1, j + 2, lambda: sent_halo(0, 1, 2, 3, 4, 5))
        matrix = sums[j + 1]
        carry_gram[0] = matrix
        for i in range(j + 1):
            hess_ref[i * width : (i + 1) * width, j * width : (j + 1) * width] = sums[i]
            hb[i] = square(sums[i])
            matrix = matrix - dot_rows(sums[i], sums[i], HIGHEST)

        def residual_part(p, j=j):
            here = pl.ds(pl.multiple_of(p * (rows // (width // 8)), rows // (width // 8)), rows // (width // 8))
            value = mf[here, :]
            for i in range(j + 1):
                value = value - halves(dot(qs[i, here, :], hb[i]))
            mf[here, :] = value

        factor(matrix, residual_part)
        hess_ref[(j + 1) * width : (j + 2) * width, j * width : (j + 1) * width] = fac[...]

    last = pltpu.make_async_copy(mf, rest_ref, out_sem.at[STEPS - 1])
    last.start()
    sent()
    inverse_ref[...] = lb[...]
    flag_ref[0, 0] = jnp.sum(cond[...])
    for j in range(1, STEPS):
        pltpu.make_async_copy(qf.at[j], bases_ref.at[j - 1], out_sem.at[j - 1]).wait()
    last.wait()


def short_form(start_block, diagonal, blocks, span_offsets, col_offsets):
    n_span, n_band = lax.axis_size("span"), lax.axis_size("band")
    nb, kc, bs, _ = blocks.shape
    rows, width = start_block.shape
    dims = (n_span, n_band, nb, bs, width, kc)
    n_xy, n_zc = n_span // 2, n_band * 2
    stride = nb + 2 * W
    nm = STEPS + 1
    chunk = width // n_xy
    vmem = pl.BlockSpec(memory_space=pltpu.VMEM)
    smem = pl.BlockSpec(memory_space=pltpu.SMEM)
    anywhere = pl.BlockSpec(memory_space=pl.ANY)

    def body(*refs):
        kernel(dims, *refs)

    return pl.pallas_call(
        body,
        out_shape=(
            jax.ShapeDtypeStruct((STEPS - 1, rows, width), F32),
            jax.ShapeDtypeStruct((rows, width), F32),
            jax.ShapeDtypeStruct((2 * width, 2 * width), BF16),
            jax.ShapeDtypeStruct(((STEPS + 1) * width, STEPS * width), F32),
            jax.ShapeDtypeStruct((width, width), F32),
            jax.ShapeDtypeStruct((1, 1), F32),
        ),
        in_specs=[vmem, vmem, anywhere, smem, smem],
        out_specs=(anywhere, anywhere, vmem, vmem, vmem, smem),
        scratch_shapes=[
            pltpu.VMEM((nb, kc, bs, bs), BF16),
            pltpu.VMEM((3 * stride, bs, width), BF16),
            pltpu.VMEM((STEPS, rows, width), F32),
            pltpu.VMEM((STEPS, rows, 2 * width), BF16),
            pltpu.VMEM((rows, width), F32),
            pltpu.VMEM((rows, width), F32),
            pltpu.VMEM((nm, 2 * width, 2 * width), F32),
            pltpu.VMEM((width, 2 * width), F32),
            pltpu.VMEM((width, width), F32),
            pltpu.VMEM((width, width), F32),
            pltpu.VMEM((10, 8, width), F32),
            pltpu.VMEM((STEPS, 2 * width, 2 * width), BF16),
            pltpu.VMEM((2 * width, 2 * width), BF16),
            pltpu.VMEM((nm, n_xy, nm, chunk, width), F32),
            pltpu.VMEM((nm, n_xy, nm, chunk, width), F32),
            pltpu.VMEM((nm, nm, chunk, width), F32),
            pltpu.VMEM((nm, n_zc, nm, chunk, width), F32),
            pltpu.VMEM((nm, nm, chunk, width), F32),
            pltpu.VMEM((nm, n_xy, nm, chunk, width), F32),
            pltpu.VMEM((1, width), F32),
            pltpu.SemaphoreType.DMA((3, max(n_xy, n_zc))),
            pltpu.SemaphoreType.DMA((2, 3, max(n_xy, n_zc))),
            pltpu.SemaphoreType.DMA((10,)),
            pltpu.SemaphoreType.DMA((10,)),
            pltpu.SemaphoreType.DMA,
            pltpu.SemaphoreType.DMA((STEPS,)),
        ],
        compiler_params=pltpu.CompilerParams(
            collective_id=0, has_side_effects=True, vmem_limit_bytes=48 * 1024 * 1024
        ),
    )(start_block, diagonal.reshape(rows // width, width), blocks, span_offsets, col_offsets)


def finish(bases, rest, inverse, hessenberg, r_first):
    before, rows, width = bases.shape
    chunks = 4
    chunk = rows // chunks

    def body(
        bases_ref, rest_ref, inverse_ref, hess_ref, first_ref, bases_to, hess_to, first_to, *scratch
    ):
        q, r, out, hess, first, in_sem, out_sem = scratch
        parts = [pl.ds(i * chunk, chunk) for i in range(chunks)]
        loads = [
            pltpu.make_async_copy(rest_ref.at[here], r.at[here], in_sem.at[i])
            for i, here in enumerate(parts)
        ]
        others = [(bases_ref.at[i], q.at[i], bases_to.at[i]) for i in range(before)]
        others += [(hess_ref, hess, hess_to), (first_ref, first, first_to)]
        for i, (source, held, _) in enumerate(others):
            loads.append(pltpu.make_async_copy(source, held, in_sem.at[chunks + i]))
        for load in loads:
            load.start()
        stores = []
        for i, here in enumerate(parts):
            loads[i].wait()
            out[here, :] = halves(dot(both(r[here, :]), inverse_ref[...]))
            stores.append(
                pltpu.make_async_copy(out.at[here], bases_to.at[before, here], out_sem.at[i])
            )
            stores[-1].start()
            if i < len(others):
                loads[chunks + i].wait()
                _, held, target = others[i]
                stores.append(pltpu.make_async_copy(held, target, out_sem.at[chunks + i]))
                stores[-1].start()
        for store in stores:
            store.wait()

    anywhere = pl.BlockSpec(memory_space=pl.ANY)
    vmem = pl.BlockSpec(memory_space=pltpu.VMEM)
    return pl.pallas_call(
        body,
        out_shape=(
            jax.ShapeDtypeStruct((before + 1, rows, width), F32),
            jax.ShapeDtypeStruct(hessenberg.shape, F32),
            jax.ShapeDtypeStruct(r_first.shape, F32),
        ),
        in_specs=[anywhere, anywhere, vmem, anywhere, anywhere],
        out_specs=(anywhere,) * 3,
        scratch_shapes=[
            pltpu.VMEM(bases.shape, F32),
            pltpu.VMEM((rows, width), F32),
            pltpu.VMEM((rows, width), F32),
            pltpu.VMEM(hessenberg.shape, F32),
            pltpu.VMEM(r_first.shape, F32),
            pltpu.SemaphoreType.DMA((chunks + before + 2,)),
            pltpu.SemaphoreType.DMA((chunks + before + 2,)),
        ],
        compiler_params=pltpu.CompilerParams(vmem_limit_bytes=16 * 1024 * 1024),
    )(bases, rest, inverse, hessenberg, r_first)


def per_device(start_block, diagonal, blocks, span_offsets, col_offsets):
    args = (start_block, diagonal, blocks, span_offsets, col_offsets)
    *parts, spread = short_form(*args)
    return lax.cond(
        spread[0, 0] <= LIMIT,
        lambda: finish(*parts),
        lambda: plain_form(*args),
    )


def solution(mesh):
    placed = (
        P(("span", "band"), None),
        P(("span", "band")),
        P(("span", "band"), None, None, None),
        P(("span", "band"), None),
        P(("span", "band"), None),
    )
    return jax.shard_map(
        per_device,
        mesh=mesh,
        in_specs=placed,
        out_specs=(P(None, ("span", "band"), None), P(), P()),
        check_vma=False,
    )
```

```python
import math

import jax
import jax.numpy as jnp
from jax import lax
from jax.experimental import pallas as pl
from jax.experimental.pallas import tpu as pltpu
from jax.sharding import PartitionSpec as P

W = 2
STEPS = 3
LIMIT = 16384.0
TALL = 2
F32 = jnp.float32
BF16 = jnp.bfloat16
MESH = pl.DeviceIdType.MESH
HIGHEST = lax.Precision.HIGHEST


def padded(block, sides, width):
    for axis, dim in sides:
        count = lax.axis_size(axis)
        forward = [(i, i + 1) for i in range(count - 1)]
        backward = [(target, source) for source, target in forward]
        low = lax.ppermute(
            lax.slice_in_dim(block, block.shape[dim] - width, None, axis=dim), axis, forward
        )
        high = lax.ppermute(lax.slice_in_dim(block, 0, width, axis=dim), axis, backward)
        block = jnp.concatenate([low, block, high], axis=dim)
    return block


def local_inner(first, second, row_total):
    return (
        jnp.dot(first.T, second, precision=HIGHEST, preferred_element_type=jnp.float32) / row_total
    )


def sum_all(value):
    for axis in ("band", "span"):
        count = lax.axis_size(axis)
        bit = 1
        while bit < count:
            value = value + lax.ppermute(value, axis, [(i, i ^ bit) for i in range(count)])
            bit *= 2
    return value


def from_upper(upper_fac, matrix):
    identity = jnp.eye(upper_fac.shape[0], dtype=jnp.float32)
    inverse = jax.scipy.linalg.solve_triangular(upper_fac.T, identity, lower=True)
    return jnp.dot(matrix, inverse.T, precision=HIGHEST, preferred_element_type=jnp.float32)


def from_gram(gram_mat, matrix):
    upper_fac = jnp.linalg.cholesky(gram_mat).T
    return (upper_fac, from_upper(upper_fac, matrix))


def apply_operator(vector, diagonal, blocks, span_offsets, col_offsets):
    block_count = blocks.shape[0]
    block_size = blocks.shape[2]
    vec_width = vector.shape[1]
    lowered = vector.astype(jnp.bfloat16).reshape(1, block_count, block_size * vec_width)
    face_cells = padded(lowered, (("span", 0),), 1)
    extended = padded(face_cells, (("band", 1),), W)
    stride = block_count + 2 * W
    lookup = extended.reshape(3 * stride, block_size, vec_width)
    row_ids = jnp.arange(block_count, dtype=jnp.int32)[:, None]
    flat_index = (span_offsets + 1) * stride + row_ids + W + col_offsets
    picked = jnp.take(lookup, flat_index, axis=0)
    coupled = jnp.einsum("ikab,ikbc->iac", blocks, picked, preferred_element_type=jnp.float32)
    return diagonal[:, None] * vector + coupled.reshape(block_count * block_size, vec_width)


def subtract_projections(mapped, bases, coeffs):
    residual = mapped
    for position in range(len(bases)):
        residual = residual - jnp.dot(
            bases[position],
            coeffs[position],
            precision=HIGHEST,
            preferred_element_type=jnp.float32,
        )
    return residual


def plain_form(start_block, diagonal, blocks, span_offsets, col_offsets):
    row_total = float(start_block.shape[0] * lax.axis_size("span") * lax.axis_size("band"))
    vec_width = start_block.shape[1]
    first_gram = sum_all(local_inner(start_block, start_block, row_total))
    r_first, current = from_gram(first_gram, start_block)
    bases = [current]
    columns = []
    for step_id in range(STEPS):
        mapped = apply_operator(bases[-1], diagonal, blocks, span_offsets, col_offsets)
        partials = jnp.stack([local_inner(earlier, mapped, row_total) for earlier in bases])
        coeffs = sum_all(partials)
        residual = subtract_projections(mapped, bases, coeffs)
        gram_mat = sum_all(local_inner(residual, residual, row_total))
        r_next, q_next = from_gram(gram_mat, residual)
        pieces = [coeffs.reshape(len(bases) * vec_width, vec_width), r_next]
        if STEPS - 1 - step_id > 0:
            pieces.append(jnp.zeros(((STEPS - 1 - step_id) * vec_width, vec_width), jnp.float32))
        columns.append(jnp.concatenate(pieces, axis=0))
        bases.append(q_next)
    hessenberg = jnp.concatenate(columns, axis=1)
    bases_out = jnp.stack(bases[1:])
    return (bases_out, hessenberg, r_first)


def dot(a, b):
    return jnp.dot(a, b, preferred_element_type=F32)


def dot_rows(a, b, precision=None):
    return lax.dot_general(
        a, b, (((0,), (0,)), ((), ())), precision=precision, preferred_element_type=F32
    )


def rounded(x):
    return x.astype(BF16).astype(F32)


def split2(x):
    high = x.astype(BF16)
    return high, (x - high.astype(F32)).astype(BF16)


def both(x):
    return jnp.concatenate(split2(x), axis=1)


def square(x):
    pair = both(x)
    return jnp.concatenate([pair, pair], axis=0)


def halves(x):
    n = x.shape[1] // 2
    return x[:, :n] + x[:, n:]


def quarters(x):
    n = x.shape[0] // 2
    return halves(x[:n] + x[n:])


def kernel(
    dims,
    start_ref,
    diag_ref,
    blocks_ref,
    spans_ref,
    cols_ref,
    bases_ref,
    rest_ref,
    inverse_ref,
    hess_ref,
    first_ref,
    flag_ref,
    blk,
    ext,
    qf,
    qs,
    mf,
    dg,
    gram,
    work,
    fac,
    inv,
    spread,
    hb,
    lb,
    part,
    recv1,
    mid,
    recv2,
    fin,
    total,
    cond,
    send_sem,
    recv_sem,
    halo_send,
    halo_recv,
    blk_sem,
    out_sem,
):
    n_span, n_band, nb, bs, width, kc = dims
    n_xy, n_zc = n_span // 2, n_band * 2
    rows = nb * bs
    stride = nb + 2 * W
    chunk = width // n_xy
    tall = rows // TALL
    scale = 1.0 / (rows * n_span * n_band)
    s = lax.axis_index("span")
    z = lax.axis_index("band")
    xy, core = s // 2, s % 2
    zc = z * 2 + core

    def xy_peer(d):
        peer = lax.rem(xy + d, n_xy)
        return peer, (peer * 2 + core, z)

    def zc_peer(d):
        peer = lax.rem(zc + d, n_zc)
        return peer, (xy * 2 + lax.rem(peer, 2), peer // 2)

    side = math.isqrt(n_xy)
    x, y = xy // side, xy % side

    def hops(step, count):
        return min(step, count - step)

    def xy_far(act):
        steps = [(dx, dy) for dx in range(side) for dy in range(side) if dx or dy]
        for dx, dy in sorted(steps, key=lambda t: -hops(t[0], side) - hops(t[1], side)):
            peer = lax.rem(x + dx, side) * side + lax.rem(y + dy, side)
            act((peer, (peer * 2 + core, z)))

    def zc_far(act):
        steps = [(dz, dc) for dz in range(n_band) for dc in range(2) if dz or dc]
        for dz, dc in sorted(steps, key=lambda t: -2 * hops(t[0], n_band) - t[1]):
            to_z, to_core = lax.rem(z + dz, n_band), lax.rem(core + dc, 2)
            act((to_z * 2 + to_core, (xy * 2 + to_core, to_z)))

    sibling, beyond = s + 1 - 2 * core, s - 1 + 2 * core
    has_beyond = (beyond >= 0) & (beyond < n_span)
    has_below, has_above = z > 0, z < n_band - 1
    near_seg, far_seg = (2 - 2 * core) * stride, 2 * core * stride
    always = z >= 0
    low, high = W, nb
    top = nb + W

    moves = [
        (stride + low, near_seg + low, W, (beyond, z), has_beyond, far_seg + low, has_beyond),
        (stride + high, near_seg + high, W, (beyond, z), has_beyond, far_seg + high, has_beyond),
        (stride + low, stride + top, W, (s, z - 1), has_below, stride + top, has_above),
        (stride + high, stride, W, (s, z + 1), has_above, stride, has_below),
        (stride + low, far_seg + low, nb, (sibling, z), always, near_seg + low, always),
        (
            stride + low + W,
            near_seg + low + W,
            nb - 2 * W,
            (beyond, z),
            has_beyond,
            far_seg + low + W,
            has_beyond,
        ),
        (stride, far_seg, W, (sibling, z), has_below, near_seg, has_below),
        (stride + top, far_seg + top, W, (sibling, z), has_above, near_seg + top, has_above),
        (
            far_seg + high,
            far_seg,
            W,
            (s, z + 1),
            has_beyond & has_above,
            far_seg,
            has_beyond & has_below,
        ),
        (
            far_seg + low,
            far_seg + top,
            W,
            (s, z - 1),
            has_beyond & has_below,
            far_seg + top,
            has_beyond & has_above,
        ),
    ]

    def move(n, source, target, count, device):
        return pltpu.make_async_remote_copy(
            src_ref=ext.at[pl.ds(source, count)],
            dst_ref=ext.at[pl.ds(target, count)],
            send_sem=halo_send.at[n],
            recv_sem=halo_recv.at[n],
            device_id=device,
            device_id_type=MESH,
        )

    def send(*chosen):
        for n in chosen:
            source, target, count, device, goes, _, _ = moves[n]

            @pl.when(goes)
            def _():
                move(n, source, target, count, device).start()

    def sent_halo(*chosen):
        for n in chosen:
            source, target, count, device, goes, _, _ = moves[n]

            @pl.when(goes)
            def _():
                move(n, source, target, count, device).wait_send()

    def arrived(*chosen):
        for n in chosen:
            source, _, count, device, _, here, comes = moves[n]

            @pl.when(comes)
            def _():
                move(n, source, here, count, device).wait_recv()

    barrier = pltpu.get_barrier_semaphore()

    def greet(peer_of):
        def body(d, carry):
            pl.semaphore_signal(barrier, inc=1, device_id=peer_of(d)[1], device_id_type=MESH)
            return carry

        return body

    lax.fori_loop(1, n_xy, greet(xy_peer), 0)
    lax.fori_loop(1, n_zc, greet(zc_peer), 0)

    @pl.when(has_beyond)
    def _():
        pl.semaphore_signal(barrier, inc=1, device_id=(beyond, z), device_id_type=MESH)

    load = pltpu.make_async_copy(blocks_ref, blk, blk_sem)
    load.start()

    def products(bases):
        nm = bases + 1
        for i in range(rows // tall):
            here = pl.ds(i * tall, tall)
            pair = both(mf[here, :])
            lefts = jnp.concatenate([qs[m, here, :] for m in range(bases)] + [pair], axis=1)
            value = dot_rows(lefts, pair).reshape(nm, 2 * width, 2 * width)
            gram[:nm] = value if i == 0 else gram[:nm] + value

    def publish(t, nm):
        for m in range(nm):
            part[t, :, m] = (quarters(gram[m]) * scale).reshape(n_xy, chunk, width)

    def all_reduce(t, nm, meanwhile=None):
        take = pl.ds(0, nm)
        par = t % 2

        def copy(stage, source, target, device):
            return pltpu.make_async_remote_copy(
                src_ref=source,
                dst_ref=target,
                send_sem=send_sem.at[stage],
                recv_sem=recv_sem.at[par, stage],
                device_id=device,
                device_id_type=MESH,
            )

        def landed(stage, buffer, count):
            pieces = buffer.at[t, pl.ds(0, count - 1), take]
            copy(stage, pieces, pieces, (sibling, z)).wait_recv()

        def left(stage, buffer, count):
            pieces = buffer.at[t, pl.ds(0, count - 1), take]
            copy(stage, pieces, pieces, (sibling, z)).wait_send()

        xy_far(lambda who: copy(0, part.at[t, who[0], take], recv1.at[t, xy, take], who[1]).start())
        recv1[t, xy, :nm] = part[t, xy, :nm]
        if meanwhile is not None:
            meanwhile()
        landed(0, recv1, n_xy)
        value = recv1[t, 0, :nm]
        for i in range(1, n_xy):
            value = value + recv1[t, i, :nm]
        mid[t, :nm] = value
        zc_far(lambda who: copy(1, mid.at[t, take], recv2.at[t, zc, take], who[1]).start())
        recv2[t, zc, :nm] = value
        landed(1, recv2, n_zc)
        value = recv2[t, 0, :nm]
        for i in range(1, n_zc):
            value = value + recv2[t, i, :nm]
        fin[t, :nm] = value
        xy_far(lambda who: copy(2, fin.at[t, take], total.at[t, xy, take], who[1]).start())
        total[t, xy, :nm] = value
        landed(2, total, n_xy)

        def sent():
            left(0, recv1, n_xy)
            left(1, recv2, n_zc)
            left(2, total, n_xy)

        return [total[t, :, m].reshape(width, width) for m in range(nm)], sent

    def factor(matrix, beside):
        w = width
        tile = (8, w)
        work[:, :w] = matrix
        eye = lax.broadcasted_iota(jnp.int32, (w, w), 0) == lax.broadcasted_iota(
            jnp.int32, (w, w), 1
        )
        work[:, w:] = jnp.where(eye, 1.0, 0.0).astype(F32)
        row = lax.broadcasted_iota(jnp.int32, tile, 0)
        lane = lax.broadcasted_iota(jnp.int32, tile, 1)
        lanes = lax.broadcasted_iota(jnp.int32, (w, w), 1)
        within, group = lax.rem(lanes, 8), lanes // 8
        firsts = (group == 0) | (group == 1) | (group == 4)
        seconds = (group == 2) | (group == 3)
        thirds = group == 5

        def assemble(lines):
            out = lines[7]
            for j in range(6, -1, -1):
                out = jnp.where(row == j, lines[j], out)
            return out

        def panel(p, carry):
            k0 = pl.multiple_of(p * 8, 8)
            pivot = work[pl.ds(k0, 8), :w]
            for j in range(8):
                spread[j] = jnp.take_along_axis(pivot, jnp.broadcast_to(k0 + j, tile), axis=1)
            spread[8] = pivot
            spread[9] = work[pl.ds(k0, 8), w:]
            columns = jnp.take_along_axis(work[:, :w], k0 + within, axis=1)
            a1 = rounded(columns)
            a2 = rounded(columns - a1)
            a3 = columns - a1 - a2
            left = jnp.where(firsts, a1, jnp.where(seconds, a2, jnp.where(thirds, a3, 0.0)))
            left = left.astype(BF16)[:, :48]

            def line(n, i):
                return jnp.broadcast_to(spread[n, pl.ds(i, 1), :], tile)

            a = [[line(j, i) if i >= j else None for j in range(8)] for i in range(8)]
            heads = [line(8, i) for i in range(8)]
            tails = [line(9, i) for i in range(8)]
            beside(p)
            by = [None] * 8
            for j in range(8):
                by[j] = lax.rsqrt(a[j][j])
                heads[j] = heads[j] * by[j]
                tails[j] = tails[j] * by[j]
                for i in range(j + 1, 8):
                    a[i][j] = a[i][j] * by[j]
                for i in range(j + 1, 8):
                    for m in range(j + 1, i + 1):
                        a[i][m] = a[i][m] - a[i][j] * a[m][j]
                    heads[i] = heads[i] - a[i][j] * heads[j]
                    tails[i] = tails[i] - a[i][j] * tails[j]
            fac[pl.ds(k0, 8), :] = jnp.where(lane >= k0 + row, assemble(heads), 0.0)
            inv[pl.ds(k0, 8), :] = assemble(tails)
            for j in range(7, -1, -1):
                heads[j] = heads[j] * by[j]
                tails[j] = tails[j] * by[j]
                for i in range(j):
                    heads[i] = heads[i] - a[j][i] * heads[j]
                    tails[i] = tails[i] - a[j][i] * tails[j]
            right = jnp.concatenate([assemble(heads), assemble(tails)], axis=1)
            b1 = rounded(right)
            b2 = rounded(right - b1)
            b3 = right - b1 - b2
            rights = jnp.concatenate([b1, b2, b1, b2, b3, b1], axis=0).astype(BF16)
            work[...] = work[...] - dot(left, rights)
            return carry

        lax.fori_loop(0, w // 8, panel, 0)
        inverse = inv[...]
        lb[...] = square(inverse.T)
        diag = jnp.sum(jnp.where(eye, carry_gram[0], 0.0), axis=0, keepdims=True)
        cond[...] = cond[...] + diag * jnp.sum(inverse * inverse, axis=0, keepdims=True)

    carry_gram = [None]

    def form_basis(t):
        def form(i):
            here = pl.ds(pl.multiple_of(i * bs, bs), bs)
            q = halves(dot(both(mf[here, :]), lb[...]))
            qf[t, here, :] = q
            high, low = split2(q)
            qs[t, here, :] = jnp.concatenate([high, low], axis=1)
            ext[stride + W + i] = high

        def ends(e, carry):
            form(jnp.where(e < W, e, e + nb - 2 * W))
            return carry

        def middle(i, carry):
            form(i)
            return carry

        lax.fori_loop(0, 2 * W, ends, 0, unroll=True)
        send(0, 1, 2, 3)
        lax.fori_loop(W, nb - W, middle, 0, unroll=True)
        send(4, 5)

    cond[...] = jnp.zeros_like(cond)
    hess_ref[...] = jnp.zeros_like(hess_ref)
    mf[...] = start_ref[...]
    products(0)
    publish(0, 1)
    pl.semaphore_wait(barrier, n_xy + n_zc - 2 + has_beyond.astype(jnp.int32))

    def expand_diag():
        ext[...] = jnp.zeros_like(ext)

        def body(c, carry):
            line = jnp.broadcast_to(diag_ref[pl.ds(c, 1), :], (width, width))
            dg[pl.ds(pl.multiple_of(c * width, width), width), :] = line.T
            return carry

        lax.fori_loop(0, rows // width, body, 0)

    (matrix,), sent = all_reduce(0, 1, expand_diag)
    carry_gram[0] = matrix
    factor(matrix, lambda p: None)
    first_ref[...] = fac[...]
    load.wait()

    for j in range(STEPS):
        form_basis(j)
        if j > 0:
            pltpu.make_async_copy(qf.at[j], bases_ref.at[j - 1], out_sem.at[j - 1]).start()
        sent()
        arrived(3)
        send(6)
        arrived(2)
        send(7)
        arrived(1)
        send(8)
        arrived(0)
        send(9)
        arrived(4, 5, 6, 7, 8, 9)

        def block_row(i, carry, j=j):
            here = pl.ds(pl.multiple_of(i * bs, bs), bs)
            acc = dg[here, :] * qf[j, here, :]
            for k in range(kc):
                at = (spans_ref[i, k] + 1) * stride + i + W + cols_ref[i, k]
                acc = acc + dot(blk[i, k], ext[at])
            mf[here, :] = acc
            return carry

        lax.fori_loop(0, nb, block_row, 0, unroll=2)
        products(j + 1)
        sent_halo(6, 7, 8, 9)
        publish(j + 1, j + 2)
        sums, sent = all_reduce(j + 1, j + 2, lambda: sent_halo(0, 1, 2, 3, 4, 5))
        matrix = sums[j + 1]
        carry_gram[0] = matrix
        for i in range(j + 1):
            hess_ref[i * width : (i + 1) * width, j * width : (j + 1) * width] = sums[i]
            hb[i] = square(sums[i])
            matrix = matrix - dot_rows(sums[i], sums[i], HIGHEST)

        def residual_part(p, j=j):
            here = pl.ds(pl.multiple_of(p * (rows // (width // 8)), rows // (width // 8)), rows // (width // 8))
            value = mf[here, :]
            for i in range(j + 1):
                value = value - halves(dot(qs[i, here, :], hb[i]))
            mf[here, :] = value

        factor(matrix, residual_part)
        hess_ref[(j + 1) * width : (j + 2) * width, j * width : (j + 1) * width] = fac[...]

    last = pltpu.make_async_copy(mf, rest_ref, out_sem.at[STEPS - 1])
    last.start()
    sent()
    inverse_ref[...] = lb[...]
    flag_ref[0, 0] = jnp.sum(cond[...])
    for j in range(1, STEPS):
        pltpu.make_async_copy(qf.at[j], bases_ref.at[j - 1], out_sem.at[j - 1]).wait()
    last.wait()


def short_form(start_block, diagonal, blocks, span_offsets, col_offsets):
    n_span, n_band = lax.axis_size("span"), lax.axis_size("band")
    nb, kc, bs, _ = blocks.shape
    rows, width = start_block.shape
    dims = (n_span, n_band, nb, bs, width, kc)
    n_xy, n_zc = n_span // 2, n_band * 2
    stride = nb + 2 * W
    nm = STEPS + 1
    chunk = width // n_xy
    vmem = pl.BlockSpec(memory_space=pltpu.VMEM)
    smem = pl.BlockSpec(memory_space=pltpu.SMEM)
    anywhere = pl.BlockSpec(memory_space=pl.ANY)

    def body(*refs):
        kernel(dims, *refs)

    return pl.pallas_call(
        body,
        out_shape=(
            jax.ShapeDtypeStruct((STEPS - 1, rows, width), F32),
            jax.ShapeDtypeStruct((rows, width), F32),
            jax.ShapeDtypeStruct((2 * width, 2 * width), BF16),
            jax.ShapeDtypeStruct(((STEPS + 1) * width, STEPS * width), F32),
            jax.ShapeDtypeStruct((width, width), F32),
            jax.ShapeDtypeStruct((1, 1), F32),
        ),
        in_specs=[vmem, vmem, anywhere, smem, smem],
        out_specs=(anywhere, anywhere, vmem, vmem, vmem, smem),
        scratch_shapes=[
            pltpu.VMEM((nb, kc, bs, bs), BF16),
            pltpu.VMEM((3 * stride, bs, width), BF16),
            pltpu.VMEM((STEPS, rows, width), F32),
            pltpu.VMEM((STEPS, rows, 2 * width), BF16),
            pltpu.VMEM((rows, width), F32),
            pltpu.VMEM((rows, width), F32),
            pltpu.VMEM((nm, 2 * width, 2 * width), F32),
            pltpu.VMEM((width, 2 * width), F32),
            pltpu.VMEM((width, width), F32),
            pltpu.VMEM((width, width), F32),
            pltpu.VMEM((10, 8, width), F32),
            pltpu.VMEM((STEPS, 2 * width, 2 * width), BF16),
            pltpu.VMEM((2 * width, 2 * width), BF16),
            pltpu.VMEM((nm, n_xy, nm, chunk, width), F32),
            pltpu.VMEM((nm, n_xy, nm, chunk, width), F32),
            pltpu.VMEM((nm, nm, chunk, width), F32),
            pltpu.VMEM((nm, n_zc, nm, chunk, width), F32),
            pltpu.VMEM((nm, nm, chunk, width), F32),
            pltpu.VMEM((nm, n_xy, nm, chunk, width), F32),
            pltpu.VMEM((1, width), F32),
            pltpu.SemaphoreType.DMA((3,)),
            pltpu.SemaphoreType.DMA((2, 3)),
            pltpu.SemaphoreType.DMA((10,)),
            pltpu.SemaphoreType.DMA((10,)),
            pltpu.SemaphoreType.DMA,
            pltpu.SemaphoreType.DMA((STEPS,)),
        ],
        compiler_params=pltpu.CompilerParams(
            collective_id=0, has_side_effects=True, vmem_limit_bytes=48 * 1024 * 1024
        ),
    )(start_block, diagonal.reshape(rows // width, width), blocks, span_offsets, col_offsets)


def finish(bases, rest, inverse, hessenberg, r_first):
    before, rows, width = bases.shape
    chunks = 4
    chunk = rows // chunks

    def body(
        bases_ref, rest_ref, inverse_ref, hess_ref, first_ref, bases_to, hess_to, first_to, *scratch
    ):
        q, r, out, hess, first, in_sem, out_sem = scratch
        parts = [pl.ds(i * chunk, chunk) for i in range(chunks)]
        loads = [
            pltpu.make_async_copy(rest_ref.at[here], r.at[here], in_sem.at[i])
            for i, here in enumerate(parts)
        ]
        others = [(bases_ref.at[i], q.at[i], bases_to.at[i]) for i in range(before)]
        others += [(hess_ref, hess, hess_to), (first_ref, first, first_to)]
        for i, (source, held, _) in enumerate(others):
            loads.append(pltpu.make_async_copy(source, held, in_sem.at[chunks + i]))
        for load in loads:
            load.start()
        stores = []
        for i, here in enumerate(parts):
            loads[i].wait()
            out[here, :] = halves(dot(both(r[here, :]), inverse_ref[...]))
            stores.append(
                pltpu.make_async_copy(out.at[here], bases_to.at[before, here], out_sem.at[i])
            )
            stores[-1].start()
            if i < len(others):
                loads[chunks + i].wait()
                _, held, target = others[i]
                stores.append(pltpu.make_async_copy(held, target, out_sem.at[chunks + i]))
                stores[-1].start()
        for store in stores:
            store.wait()

    anywhere = pl.BlockSpec(memory_space=pl.ANY)
    vmem = pl.BlockSpec(memory_space=pltpu.VMEM)
    return pl.pallas_call(
        body,
        out_shape=(
            jax.ShapeDtypeStruct((before + 1, rows, width), F32),
            jax.ShapeDtypeStruct(hessenberg.shape, F32),
            jax.ShapeDtypeStruct(r_first.shape, F32),
        ),
        in_specs=[anywhere, anywhere, vmem, anywhere, anywhere],
        out_specs=(anywhere,) * 3,
        scratch_shapes=[
            pltpu.VMEM(bases.shape, F32),
            pltpu.VMEM((rows, width), F32),
            pltpu.VMEM((rows, width), F32),
            pltpu.VMEM(hessenberg.shape, F32),
            pltpu.VMEM(r_first.shape, F32),
            pltpu.SemaphoreType.DMA((chunks + before + 2,)),
            pltpu.SemaphoreType.DMA((chunks + before + 2,)),
        ],
        compiler_params=pltpu.CompilerParams(vmem_limit_bytes=16 * 1024 * 1024),
    )(bases, rest, inverse, hessenberg, r_first)


def per_device(start_block, diagonal, blocks, span_offsets, col_offsets):
    args = (start_block, diagonal, blocks, span_offsets, col_offsets)
    *parts, spread = short_form(*args)
    return lax.cond(
        spread[0, 0] <= LIMIT,
        lambda: finish(*parts),
        lambda: plain_form(*args),
    )


def solution(mesh):
    placed = (
        P(("span", "band"), None),
        P(("span", "band")),
        P(("span", "band"), None, None, None),
        P(("span", "band"), None),
        P(("span", "band"), None),
    )
    return jax.shard_map(
        per_device,
        mesh=mesh,
        in_specs=placed,
        out_specs=(P(None, ("span", "band"), None), P(), P()),
        check_vma=False,
    )
```

```python
import math

import jax
import jax.numpy as jnp
from jax import lax
from jax.experimental import pallas as pl
from jax.experimental.pallas import tpu as pltpu
from jax.sharding import PartitionSpec as P

W = 2
STEPS = 3
LIMIT = 16384.0
TALL = 2
F32 = jnp.float32
BF16 = jnp.bfloat16
MESH = pl.DeviceIdType.MESH
HIGHEST = lax.Precision.HIGHEST


def padded(block, sides, width):
    for axis, dim in sides:
        count = lax.axis_size(axis)
        forward = [(i, i + 1) for i in range(count - 1)]
        backward = [(target, source) for source, target in forward]
        low = lax.ppermute(
            lax.slice_in_dim(block, block.shape[dim] - width, None, axis=dim), axis, forward
        )
        high = lax.ppermute(lax.slice_in_dim(block, 0, width, axis=dim), axis, backward)
        block = jnp.concatenate([low, block, high], axis=dim)
    return block


def local_inner(first, second, row_total):
    return (
        jnp.dot(first.T, second, precision=HIGHEST, preferred_element_type=jnp.float32) / row_total
    )


def sum_all(value):
    for axis in ("band", "span"):
        count = lax.axis_size(axis)
        bit = 1
        while bit < count:
            value = value + lax.ppermute(value, axis, [(i, i ^ bit) for i in range(count)])
            bit *= 2
    return value


def from_upper(upper_fac, matrix):
    identity = jnp.eye(upper_fac.shape[0], dtype=jnp.float32)
    inverse = jax.scipy.linalg.solve_triangular(upper_fac.T, identity, lower=True)
    return jnp.dot(matrix, inverse.T, precision=HIGHEST, preferred_element_type=jnp.float32)


def from_gram(gram_mat, matrix):
    upper_fac = jnp.linalg.cholesky(gram_mat).T
    return (upper_fac, from_upper(upper_fac, matrix))


def apply_operator(vector, diagonal, blocks, span_offsets, col_offsets):
    block_count = blocks.shape[0]
    block_size = blocks.shape[2]
    vec_width = vector.shape[1]
    lowered = vector.astype(jnp.bfloat16).reshape(1, block_count, block_size * vec_width)
    face_cells = padded(lowered, (("span", 0),), 1)
    extended = padded(face_cells, (("band", 1),), W)
    stride = block_count + 2 * W
    lookup = extended.reshape(3 * stride, block_size, vec_width)
    row_ids = jnp.arange(block_count, dtype=jnp.int32)[:, None]
    flat_index = (span_offsets + 1) * stride + row_ids + W + col_offsets
    picked = jnp.take(lookup, flat_index, axis=0)
    coupled = jnp.einsum("ikab,ikbc->iac", blocks, picked, preferred_element_type=jnp.float32)
    return diagonal[:, None] * vector + coupled.reshape(block_count * block_size, vec_width)


def subtract_projections(mapped, bases, coeffs):
    residual = mapped
    for position in range(len(bases)):
        residual = residual - jnp.dot(
            bases[position],
            coeffs[position],
            precision=HIGHEST,
            preferred_element_type=jnp.float32,
        )
    return residual


def plain_form(start_block, diagonal, blocks, span_offsets, col_offsets):
    row_total = float(start_block.shape[0] * lax.axis_size("span") * lax.axis_size("band"))
    vec_width = start_block.shape[1]
    first_gram = sum_all(local_inner(start_block, start_block, row_total))
    r_first, current = from_gram(first_gram, start_block)
    bases = [current]
    columns = []
    for step_id in range(STEPS):
        mapped = apply_operator(bases[-1], diagonal, blocks, span_offsets, col_offsets)
        partials = jnp.stack([local_inner(earlier, mapped, row_total) for earlier in bases])
        coeffs = sum_all(partials)
        residual = subtract_projections(mapped, bases, coeffs)
        gram_mat = sum_all(local_inner(residual, residual, row_total))
        r_next, q_next = from_gram(gram_mat, residual)
        pieces = [coeffs.reshape(len(bases) * vec_width, vec_width), r_next]
        if STEPS - 1 - step_id > 0:
            pieces.append(jnp.zeros(((STEPS - 1 - step_id) * vec_width, vec_width), jnp.float32))
        columns.append(jnp.concatenate(pieces, axis=0))
        bases.append(q_next)
    hessenberg = jnp.concatenate(columns, axis=1)
    bases_out = jnp.stack(bases[1:])
    return (bases_out, hessenberg, r_first)


def dot(a, b):
    return jnp.dot(a, b, preferred_element_type=F32)


def dot_rows(a, b, precision=None):
    return lax.dot_general(
        a, b, (((0,), (0,)), ((), ())), precision=precision, preferred_element_type=F32
    )


def rounded(x):
    return x.astype(BF16).astype(F32)


def split2(x):
    high = x.astype(BF16)
    return high, (x - high.astype(F32)).astype(BF16)


def both(x):
    return jnp.concatenate(split2(x), axis=1)


def square(x):
    pair = both(x)
    return jnp.concatenate([pair, pair], axis=0)


def halves(x):
    n = x.shape[1] // 2
    return x[:, :n] + x[:, n:]


def quarters(x):
    n = x.shape[0] // 2
    return halves(x[:n] + x[n:])


def kernel(
    dims,
    start_ref,
    diag_ref,
    blocks_ref,
    spans_ref,
    cols_ref,
    bases_ref,
    rest_ref,
    inverse_ref,
    hess_ref,
    first_ref,
    flag_ref,
    hess,
    first,
    blk,
    ext,
    qf,
    qs,
    mf,
    dg,
    gram,
    work,
    fac,
    inv,
    spread,
    hb,
    lb,
    part,
    recv1,
    mid,
    recv2,
    fin,
    total,
    cond,
    send_sem,
    recv_sem,
    halo_send,
    halo_recv,
    blk_sem,
    out_sem,
):
    n_span, n_band, nb, bs, width, kc = dims
    n_xy, n_zc = n_span // 2, n_band * 2
    rows = nb * bs
    stride = nb + 2 * W
    chunk = width // n_xy
    tall = rows // TALL
    scale = 1.0 / (rows * n_span * n_band)
    s = lax.axis_index("span")
    z = lax.axis_index("band")
    xy, core = s // 2, s % 2
    zc = z * 2 + core

    def xy_peer(d):
        peer = lax.rem(xy + d, n_xy)
        return peer, (peer * 2 + core, z)

    def zc_peer(d):
        peer = lax.rem(zc + d, n_zc)
        return peer, (xy * 2 + lax.rem(peer, 2), peer // 2)

    side = math.isqrt(n_xy)
    x, y = xy // side, xy % side

    def hops(step, count):
        return min(step, count - step)

    def xy_far(act):
        steps = [(dx, dy) for dx in range(side) for dy in range(side) if dx or dy]
        for dx, dy in sorted(steps, key=lambda t: -hops(t[0], side) - hops(t[1], side)):
            peer = lax.rem(x + dx, side) * side + lax.rem(y + dy, side)
            act((peer, (peer * 2 + core, z)))

    def zc_far(act):
        steps = [(dz, dc) for dz in range(n_band) for dc in range(2) if dz or dc]
        for dz, dc in sorted(steps, key=lambda t: -2 * hops(t[0], n_band) - t[1]):
            to_z, to_core = lax.rem(z + dz, n_band), lax.rem(core + dc, 2)
            act((to_z * 2 + to_core, (xy * 2 + to_core, to_z)))

    sibling, beyond = s + 1 - 2 * core, s - 1 + 2 * core
    has_beyond = (beyond >= 0) & (beyond < n_span)
    has_below, has_above = z > 0, z < n_band - 1
    near_seg, far_seg = (2 - 2 * core) * stride, 2 * core * stride
    always = z >= 0
    low, high = W, nb
    top = nb + W

    moves = [
        (stride + low, near_seg + low, W, (beyond, z), has_beyond, far_seg + low, has_beyond),
        (stride + high, near_seg + high, W, (beyond, z), has_beyond, far_seg + high, has_beyond),
        (stride + low, stride + top, W, (s, z - 1), has_below, stride + top, has_above),
        (stride + high, stride, W, (s, z + 1), has_above, stride, has_below),
        (stride + low, far_seg + low, nb, (sibling, z), always, near_seg + low, always),
        (
            stride + low + W,
            near_seg + low + W,
            nb - 2 * W,
            (beyond, z),
            has_beyond,
            far_seg + low + W,
            has_beyond,
        ),
        (stride, far_seg, W, (sibling, z), has_below, near_seg, has_below),
        (stride + top, far_seg + top, W, (sibling, z), has_above, near_seg + top, has_above),
        (
            far_seg + high,
            far_seg,
            W,
            (s, z + 1),
            has_beyond & has_above,
            far_seg,
            has_beyond & has_below,
        ),
        (
            far_seg + low,
            far_seg + top,
            W,
            (s, z - 1),
            has_beyond & has_below,
            far_seg + top,
            has_beyond & has_above,
        ),
    ]

    def move(n, source, target, count, device):
        return pltpu.make_async_remote_copy(
            src_ref=ext.at[pl.ds(source, count)],
            dst_ref=ext.at[pl.ds(target, count)],
            send_sem=halo_send.at[n],
            recv_sem=halo_recv.at[n],
            device_id=device,
            device_id_type=MESH,
        )

    def send(*chosen):
        for n in chosen:
            source, target, count, device, goes, _, _ = moves[n]

            @pl.when(goes)
            def _():
                move(n, source, target, count, device).start()

    def sent_halo(*chosen):
        for n in chosen:
            source, target, count, device, goes, _, _ = moves[n]

            @pl.when(goes)
            def _():
                move(n, source, target, count, device).wait_send()

    def arrived(*chosen):
        for n in chosen:
            source, _, count, device, _, here, comes = moves[n]

            @pl.when(comes)
            def _():
                move(n, source, here, count, device).wait_recv()

    first_load = pltpu.make_async_copy(start_ref, mf, blk_sem.at[0])
    first_load.start()
    load = pltpu.make_async_copy(blocks_ref, blk, blk_sem.at[1])
    barrier = pltpu.get_barrier_semaphore()

    def greet(peer_of):
        def body(d, carry):
            pl.semaphore_signal(barrier, inc=1, device_id=peer_of(d)[1], device_id_type=MESH)
            return carry

        return body

    lax.fori_loop(1, n_xy, greet(xy_peer), 0)
    lax.fori_loop(1, n_zc, greet(zc_peer), 0)

    @pl.when(has_beyond)
    def _():
        pl.semaphore_signal(barrier, inc=1, device_id=(beyond, z), device_id_type=MESH)

    load.start()

    def products(bases):
        nm = bases + 1
        for i in range(rows // tall):
            here = pl.ds(i * tall, tall)
            pair = both(mf[here, :])
            lefts = jnp.concatenate([qs[m, here, :] for m in range(bases)] + [pair], axis=1)
            value = dot_rows(lefts, pair).reshape(nm, 2 * width, 2 * width)
            gram[:nm] = value if i == 0 else gram[:nm] + value

    def publish(t, nm):
        for m in range(nm):
            part[t, :, m] = (quarters(gram[m]) * scale).reshape(n_xy, chunk, width)

    def all_reduce(t, nm, meanwhile=None):
        take = pl.ds(0, nm)
        par = t % 2

        def copy(stage, source, target, device):
            return pltpu.make_async_remote_copy(
                src_ref=source,
                dst_ref=target,
                send_sem=send_sem.at[stage],
                recv_sem=recv_sem.at[par, stage],
                device_id=device,
                device_id_type=MESH,
            )

        def landed(stage, buffer, count):
            pieces = buffer.at[t, pl.ds(0, count - 1), take]
            copy(stage, pieces, pieces, (sibling, z)).wait_recv()

        def left(stage, buffer, count):
            pieces = buffer.at[t, pl.ds(0, count - 1), take]
            copy(stage, pieces, pieces, (sibling, z)).wait_send()

        xy_far(lambda who: copy(0, part.at[t, who[0], take], recv1.at[t, xy, take], who[1]).start())
        recv1[t, xy, :nm] = part[t, xy, :nm]
        if meanwhile is not None:
            meanwhile()
        landed(0, recv1, n_xy)
        value = recv1[t, 0, :nm]
        for i in range(1, n_xy):
            value = value + recv1[t, i, :nm]
        mid[t, :nm] = value
        zc_far(lambda who: copy(1, mid.at[t, take], recv2.at[t, zc, take], who[1]).start())
        recv2[t, zc, :nm] = value
        landed(1, recv2, n_zc)
        value = recv2[t, 0, :nm]
        for i in range(1, n_zc):
            value = value + recv2[t, i, :nm]
        fin[t, :nm] = value
        xy_far(lambda who: copy(2, fin.at[t, take], total.at[t, xy, take], who[1]).start())
        total[t, xy, :nm] = value
        landed(2, total, n_xy)

        def sent():
            left(0, recv1, n_xy)
            left(1, recv2, n_zc)
            left(2, total, n_xy)

        return [total[t, :, m].reshape(width, width) for m in range(nm)], sent

    def factor(matrix, beside):
        w = width
        tile = (8, w)
        work[:, :w] = matrix
        eye = lax.broadcasted_iota(jnp.int32, (w, w), 0) == lax.broadcasted_iota(
            jnp.int32, (w, w), 1
        )
        work[:, w:] = jnp.where(eye, 1.0, 0.0).astype(F32)
        row = lax.broadcasted_iota(jnp.int32, tile, 0)
        place = lax.broadcasted_iota(jnp.int32, (16, w), 0)
        lane = lax.broadcasted_iota(jnp.int32, (16, w), 1)
        lanes = lax.broadcasted_iota(jnp.int32, (w, w), 1)
        within, group = lax.rem(lanes, 16), lanes // 16
        firsts = (group == 0) | (group == 1) | (group == 4)
        seconds = (group == 2) | (group == 3)
        thirds = group == 5

        def assemble(lines):
            out = lines[7]
            for j in range(6, -1, -1):
                out = jnp.where(row == j, lines[j], out)
            return out

        def line(n, i):
            return jnp.broadcast_to(spread[n, pl.ds(i, 1), :], tile)

        def lines(n):
            return [line(n, i) for i in range(8)]

        def triangle(n):
            return [[line(n + j, i) if i >= j else None for j in range(8)] for i in range(8)]

        def eliminate(a, heads, tails, below):
            by = [None] * 8
            for j in range(8):
                by[j] = lax.rsqrt(a[j][j])
                heads[j] = heads[j] * by[j]
                tails[j] = tails[j] * by[j]
                for i in range(j + 1, 8):
                    a[i][j] = a[i][j] * by[j]
                if below:
                    below[j] = below[j] * by[j]
                for i in range(j + 1, 8):
                    for m in range(j + 1, i + 1):
                        a[i][m] = a[i][m] - a[i][j] * a[m][j]
                    heads[i] = heads[i] - a[i][j] * heads[j]
                    tails[i] = tails[i] - a[i][j] * tails[j]
                    if below:
                        below[i] = below[i] - below[j] * a[i][j]
            return by

        def substitute(a, by, heads, tails):
            for j in range(7, -1, -1):
                heads[j] = heads[j] * by[j]
                tails[j] = tails[j] * by[j]
                for i in range(j):
                    heads[i] = heads[i] - a[j][i] * heads[j]
                    tails[i] = tails[i] - a[j][i] * tails[j]

        def panel(p, carry):
            k0 = pl.multiple_of(p * 16, 16)
            upper = work[pl.ds(k0, 8), :w]
            lower = work[pl.ds(k0 + 8, 8), :w]

            def column(rows_of, j):
                return jnp.take_along_axis(rows_of, jnp.broadcast_to(k0 + j, tile), axis=1)

            for j in range(8):
                spread[j] = column(upper, j)
            below = [column(lower, j) for j in range(8)]
            block = [column(lower, 8 + j) for j in range(8)]
            spread[8] = upper
            spread[9] = work[pl.ds(k0, 8), w:]
            columns = jnp.take_along_axis(work[:, :w], k0 + within, axis=1)
            a1 = rounded(columns)
            a2 = rounded(columns - a1)
            a3 = columns - a1 - a2
            left = jnp.where(firsts, a1, jnp.where(seconds, a2, jnp.where(thirds, a3, 0.0)))
            left = left.astype(BF16)[:, :96]
            beside(p)
            a, heads, tails = triangle(0), lines(8), lines(9)
            by = eliminate(a, heads, tails, below)
            lower_tail = work[pl.ds(k0 + 8, 8), w:]
            for m in range(8):
                spread[10 + m] = below[m]
                lower = lower - below[m] * heads[m]
                lower_tail = lower_tail - below[m] * tails[m]
            cross = [[line(10 + m, i) for m in range(8)] for i in range(8)]
            for j in range(8):
                for m in range(8):
                    block[j] = block[j] - below[m] * cross[j][m]
                spread[18 + j] = block[j]
            spread[26] = lower
            spread[27] = lower_tail
            b, heads2, tails2 = triangle(18), lines(26), lines(27)
            by2 = eliminate(b, heads2, tails2, None)

            def stacked(first, second):
                return jnp.concatenate([assemble(first), assemble(second)], axis=0)

            fac[pl.ds(k0, 16), :] = jnp.where(lane >= k0 + place, stacked(heads, heads2), 0.0)
            inv[pl.ds(k0, 16), :] = stacked(tails, tails2)
            substitute(b, by2, heads2, tails2)
            for j in range(8):
                for i in range(7, -1, -1):
                    heads[j] = heads[j] - cross[i][j] * heads2[i]
                    tails[j] = tails[j] - cross[i][j] * tails2[i]
            substitute(a, by, heads, tails)
            right = jnp.concatenate([stacked(heads, heads2), stacked(tails, tails2)], axis=1)
            b1 = rounded(right)
            b2 = rounded(right - b1)
            b3 = right - b1 - b2
            rights = jnp.concatenate([b1, b2, b1, b2, b3, b1], axis=0).astype(BF16)
            work[...] = work[...] - dot(left, rights)
            return carry

        lax.fori_loop(0, w // 16, panel, 0)
        inverse = inv[...]
        lb[...] = square(inverse.T)
        diag = jnp.sum(jnp.where(eye, carry_gram[0], 0.0), axis=0, keepdims=True)
        cond[...] = cond[...] + diag * jnp.sum(inverse * inverse, axis=0, keepdims=True)

    carry_gram = [None]

    def form_basis(t):
        def form(i):
            here = pl.ds(pl.multiple_of(i * bs, bs), bs)
            q = halves(dot(both(mf[here, :]), lb[...]))
            qf[t, here, :] = q
            high, low = split2(q)
            qs[t, here, :] = jnp.concatenate([high, low], axis=1)
            ext[stride + W + i] = high

        def ends(e, carry):
            form(jnp.where(e < W, e, e + nb - 2 * W))
            return carry

        def middle(i, carry):
            form(i)
            return carry

        lax.fori_loop(0, 2 * W, ends, 0, unroll=True)
        send(0, 1, 2, 3)
        lax.fori_loop(W, nb - W, middle, 0, unroll=True)
        send(4, 5)

    cond[...] = jnp.zeros_like(cond)
    first_load.wait()
    products(0)
    publish(0, 1)
    pl.semaphore_wait(barrier, n_xy + n_zc - 2 + has_beyond.astype(jnp.int32))

    def expand_diag():
        ext[...] = jnp.zeros_like(ext)
        hess[...] = jnp.zeros_like(hess)

        def body(c, carry):
            line = jnp.broadcast_to(diag_ref[pl.ds(c, 1), :], (width, width))
            dg[pl.ds(pl.multiple_of(c * width, width), width), :] = line.T
            return carry

        lax.fori_loop(0, rows // width, body, 0)

    (matrix,), sent = all_reduce(0, 1, expand_diag)
    carry_gram[0] = matrix
    factor(matrix, lambda p: None)
    first[...] = fac[...]
    first_out = pltpu.make_async_copy(first, first_ref, out_sem.at[STEPS + 3])
    first_out.start()
    cut = rows - 2 * (rows // (width // 16))
    early_rows, late_rows = pl.ds(0, cut), pl.ds(cut, rows - cut)
    early = pltpu.make_async_copy(mf.at[early_rows], rest_ref.at[early_rows], out_sem.at[STEPS - 1])
    load.wait()

    for j in range(STEPS):
        form_basis(j)
        if j > 0:
            pltpu.make_async_copy(qf.at[j], bases_ref.at[j - 1], out_sem.at[j - 1]).start()
        sent()
        arrived(3)
        send(6)
        arrived(2)
        send(7)
        arrived(1)
        send(8)
        arrived(0)
        send(9)
        arrived(4, 5, 6, 7, 8, 9)

        def block_row(i, carry, j=j):
            here = pl.ds(pl.multiple_of(i * bs, bs), bs)
            acc = dg[here, :] * qf[j, here, :]
            for k in range(kc):
                at = (spans_ref[i, k] + 1) * stride + i + W + cols_ref[i, k]
                acc = acc + dot(blk[i, k], ext[at])
            mf[here, :] = acc
            return carry

        lax.fori_loop(0, nb, block_row, 0, unroll=2)
        products(j + 1)
        sent_halo(6, 7, 8, 9)
        publish(j + 1, j + 2)
        sums, sent = all_reduce(j + 1, j + 2, lambda: sent_halo(0, 1, 2, 3, 4, 5))
        matrix = sums[j + 1]
        carry_gram[0] = matrix
        for i in range(j + 1):
            hess[i * width : (i + 1) * width, j * width : (j + 1) * width] = sums[i]
            hb[i] = square(sums[i])

        tallest = jnp.concatenate(sums[: j + 1], axis=0)
        matrix = matrix - dot_rows(tallest, tallest, HIGHEST)
        share = rows // (width // 16)

        def residual_part(p, j=j):
            here = pl.ds(pl.multiple_of(p * share, share), share)
            value = mf[here, :]
            for i in range(j + 1):
                value = value - halves(dot(qs[i, here, :], hb[i]))
            mf[here, :] = value
            if j == STEPS - 1:

                @pl.when(p == width // 16 - 2)
                def _():
                    early.start()

        factor(matrix, residual_part)
        hess[(j + 1) * width : (j + 2) * width, j * width : (j + 1) * width] = fac[...]

    ends = [
        pltpu.make_async_copy(mf.at[late_rows], rest_ref.at[late_rows], out_sem.at[STEPS]),
        pltpu.make_async_copy(lb, inverse_ref, out_sem.at[STEPS + 1]),
        pltpu.make_async_copy(hess, hess_ref, out_sem.at[STEPS + 2]),
    ]
    for copy in ends:
        copy.start()
    sent()
    flag_ref[0, 0] = jnp.sum(cond[...])
    for j in range(1, STEPS):
        pltpu.make_async_copy(qf.at[j], bases_ref.at[j - 1], out_sem.at[j - 1]).wait()
    early.wait()
    first_out.wait()
    for copy in ends:
        copy.wait()


def short_form(start_block, diagonal, blocks, span_offsets, col_offsets):
    n_span, n_band = lax.axis_size("span"), lax.axis_size("band")
    nb, kc, bs, _ = blocks.shape
    rows, width = start_block.shape
    dims = (n_span, n_band, nb, bs, width, kc)
    n_xy, n_zc = n_span // 2, n_band * 2
    stride = nb + 2 * W
    nm = STEPS + 1
    chunk = width // n_xy
    vmem = pl.BlockSpec(memory_space=pltpu.VMEM)
    smem = pl.BlockSpec(memory_space=pltpu.SMEM)
    anywhere = pl.BlockSpec(memory_space=pl.ANY)

    def body(*refs):
        kernel(dims, *refs)

    return pl.pallas_call(
        body,
        out_shape=(
            jax.ShapeDtypeStruct((STEPS - 1, rows, width), F32),
            jax.ShapeDtypeStruct((rows, width), F32),
            jax.ShapeDtypeStruct((2 * width, 2 * width), BF16),
            jax.ShapeDtypeStruct(((STEPS + 1) * width, STEPS * width), F32),
            jax.ShapeDtypeStruct((width, width), F32),
            jax.ShapeDtypeStruct((1, 1), F32),
        ),
        in_specs=[anywhere, vmem, anywhere, smem, smem],
        out_specs=(anywhere,) * 5 + (smem,),
        scratch_shapes=[
            pltpu.VMEM(((STEPS + 1) * width, STEPS * width), F32),
            pltpu.VMEM((width, width), F32),
            pltpu.VMEM((nb, kc, bs, bs), BF16),
            pltpu.VMEM((3 * stride, bs, width), BF16),
            pltpu.VMEM((STEPS, rows, width), F32),
            pltpu.VMEM((STEPS, rows, 2 * width), BF16),
            pltpu.VMEM((rows, width), F32),
            pltpu.VMEM((rows, width), F32),
            pltpu.VMEM((nm, 2 * width, 2 * width), F32),
            pltpu.VMEM((width, 2 * width), F32),
            pltpu.VMEM((width, width), F32),
            pltpu.VMEM((width, width), F32),
            pltpu.VMEM((28, 8, width), F32),
            pltpu.VMEM((STEPS, 2 * width, 2 * width), BF16),
            pltpu.VMEM((2 * width, 2 * width), BF16),
            pltpu.VMEM((nm, n_xy, nm, chunk, width), F32),
            pltpu.VMEM((nm, n_xy, nm, chunk, width), F32),
            pltpu.VMEM((nm, nm, chunk, width), F32),
            pltpu.VMEM((nm, n_zc, nm, chunk, width), F32),
            pltpu.VMEM((nm, nm, chunk, width), F32),
            pltpu.VMEM((nm, n_xy, nm, chunk, width), F32),
            pltpu.VMEM((1, width), F32),
            pltpu.SemaphoreType.DMA((3,)),
            pltpu.SemaphoreType.DMA((2, 3)),
            pltpu.SemaphoreType.DMA((10,)),
            pltpu.SemaphoreType.DMA((10,)),
            pltpu.SemaphoreType.DMA((2,)),
            pltpu.SemaphoreType.DMA((STEPS + 4,)),
        ],
        compiler_params=pltpu.CompilerParams(
            collective_id=0, has_side_effects=True, vmem_limit_bytes=48 * 1024 * 1024
        ),
    )(start_block, diagonal.reshape(rows // width, width), blocks, span_offsets, col_offsets)


def finish(bases, rest, inverse, hessenberg, r_first):
    before, rows, width = bases.shape
    chunks = 4
    chunk = rows // chunks

    def body(
        bases_ref, rest_ref, inverse_ref, hess_ref, first_ref, bases_to, hess_to, first_to, *scratch
    ):
        q, r, out, hess, first, in_sem, out_sem = scratch
        parts = [pl.ds(i * chunk, chunk) for i in range(chunks)]
        loads = [
            pltpu.make_async_copy(rest_ref.at[here], r.at[here], in_sem.at[i])
            for i, here in enumerate(parts)
        ]
        others = [(bases_ref.at[i], q.at[i], bases_to.at[i]) for i in range(before)]
        others += [(hess_ref, hess, hess_to), (first_ref, first, first_to)]
        for i, (source, held, _) in enumerate(others):
            loads.append(pltpu.make_async_copy(source, held, in_sem.at[chunks + i]))
        for load in loads:
            load.start()
        stores = []
        for i, here in enumerate(parts):
            loads[i].wait()
            out[here, :] = halves(dot(both(r[here, :]), inverse_ref[...]))
            stores.append(
                pltpu.make_async_copy(out.at[here], bases_to.at[before, here], out_sem.at[i])
            )
            stores[-1].start()
            if i < len(others):
                loads[chunks + i].wait()
                _, held, target = others[i]
                stores.append(pltpu.make_async_copy(held, target, out_sem.at[chunks + i]))
                stores[-1].start()
        for store in stores:
            store.wait()

    anywhere = pl.BlockSpec(memory_space=pl.ANY)
    vmem = pl.BlockSpec(memory_space=pltpu.VMEM)
    return pl.pallas_call(
        body,
        out_shape=(
            jax.ShapeDtypeStruct((before + 1, rows, width), F32),
            jax.ShapeDtypeStruct(hessenberg.shape, F32),
            jax.ShapeDtypeStruct(r_first.shape, F32),
        ),
        in_specs=[anywhere, anywhere, vmem, anywhere, anywhere],
        out_specs=(anywhere,) * 3,
        scratch_shapes=[
            pltpu.VMEM(bases.shape, F32),
            pltpu.VMEM((rows, width), F32),
            pltpu.VMEM((rows, width), F32),
            pltpu.VMEM(hessenberg.shape, F32),
            pltpu.VMEM(r_first.shape, F32),
            pltpu.SemaphoreType.DMA((chunks + before + 2,)),
            pltpu.SemaphoreType.DMA((chunks + before + 2,)),
        ],
        compiler_params=pltpu.CompilerParams(vmem_limit_bytes=16 * 1024 * 1024),
    )(bases, rest, inverse, hessenberg, r_first)


def per_device(start_block, diagonal, blocks, span_offsets, col_offsets):
    args = (start_block, diagonal, blocks, span_offsets, col_offsets)
    *parts, spread = short_form(*args)
    return lax.cond(
        spread[0, 0] <= LIMIT,
        lambda: finish(*parts),
        lambda: plain_form(*args),
    )


def solution(mesh):
    placed = (
        P(("span", "band"), None),
        P(("span", "band")),
        P(("span", "band"), None, None, None),
        P(("span", "band"), None),
        P(("span", "band"), None),
    )
    return jax.shard_map(
        per_device,
        mesh=mesh,
        in_specs=placed,
        out_specs=(P(None, ("span", "band"), None), P(), P()),
        check_vma=False,
    )
```

```python
import math

import jax
import jax.numpy as jnp
from jax import lax
from jax.experimental import pallas as pl
from jax.experimental.pallas import tpu as pltpu
from jax.sharding import PartitionSpec as P

W = 2
STEPS = 3
LIMIT = 16384.0
F32 = jnp.float32
BF16 = jnp.bfloat16
MESH = pl.DeviceIdType.MESH
HIGHEST = lax.Precision.HIGHEST


def padded(block, sides, width):
    for axis, dim in sides:
        count = lax.axis_size(axis)
        forward = [(i, i + 1) for i in range(count - 1)]
        backward = [(target, source) for source, target in forward]
        low = lax.ppermute(
            lax.slice_in_dim(block, block.shape[dim] - width, None, axis=dim), axis, forward
        )
        high = lax.ppermute(lax.slice_in_dim(block, 0, width, axis=dim), axis, backward)
        block = jnp.concatenate([low, block, high], axis=dim)
    return block


def local_inner(first, second, row_total):
    return (
        jnp.dot(first.T, second, precision=HIGHEST, preferred_element_type=jnp.float32) / row_total
    )


def sum_all(value):
    for axis in ("band", "span"):
        count = lax.axis_size(axis)
        bit = 1
        while bit < count:
            value = value + lax.ppermute(value, axis, [(i, i ^ bit) for i in range(count)])
            bit *= 2
    return value


def from_upper(upper_fac, matrix):
    identity = jnp.eye(upper_fac.shape[0], dtype=jnp.float32)
    inverse = jax.scipy.linalg.solve_triangular(upper_fac.T, identity, lower=True)
    return jnp.dot(matrix, inverse.T, precision=HIGHEST, preferred_element_type=jnp.float32)


def from_gram(gram_mat, matrix):
    upper_fac = jnp.linalg.cholesky(gram_mat).T
    return (upper_fac, from_upper(upper_fac, matrix))


def apply_operator(vector, diagonal, blocks, span_offsets, col_offsets):
    block_count = blocks.shape[0]
    block_size = blocks.shape[2]
    vec_width = vector.shape[1]
    lowered = vector.astype(jnp.bfloat16).reshape(1, block_count, block_size * vec_width)
    face_cells = padded(lowered, (("span", 0),), 1)
    extended = padded(face_cells, (("band", 1),), W)
    stride = block_count + 2 * W
    lookup = extended.reshape(3 * stride, block_size, vec_width)
    row_ids = jnp.arange(block_count, dtype=jnp.int32)[:, None]
    flat_index = (span_offsets + 1) * stride + row_ids + W + col_offsets
    picked = jnp.take(lookup, flat_index, axis=0)
    coupled = jnp.einsum("ikab,ikbc->iac", blocks, picked, preferred_element_type=jnp.float32)
    return diagonal[:, None] * vector + coupled.reshape(block_count * block_size, vec_width)


def subtract_projections(mapped, bases, coeffs):
    residual = mapped
    for position in range(len(bases)):
        residual = residual - jnp.dot(
            bases[position],
            coeffs[position],
            precision=HIGHEST,
            preferred_element_type=jnp.float32,
        )
    return residual


def plain_form(start_block, diagonal, blocks, span_offsets, col_offsets):
    row_total = float(start_block.shape[0] * lax.axis_size("span") * lax.axis_size("band"))
    vec_width = start_block.shape[1]
    first_gram = sum_all(local_inner(start_block, start_block, row_total))
    r_first, current = from_gram(first_gram, start_block)
    bases = [current]
    columns = []
    for step_id in range(STEPS):
        mapped = apply_operator(bases[-1], diagonal, blocks, span_offsets, col_offsets)
        partials = jnp.stack([local_inner(earlier, mapped, row_total) for earlier in bases])
        coeffs = sum_all(partials)
        residual = subtract_projections(mapped, bases, coeffs)
        gram_mat = sum_all(local_inner(residual, residual, row_total))
        r_next, q_next = from_gram(gram_mat, residual)
        pieces = [coeffs.reshape(len(bases) * vec_width, vec_width), r_next]
        if STEPS - 1 - step_id > 0:
            pieces.append(jnp.zeros(((STEPS - 1 - step_id) * vec_width, vec_width), jnp.float32))
        columns.append(jnp.concatenate(pieces, axis=0))
        bases.append(q_next)
    hessenberg = jnp.concatenate(columns, axis=1)
    bases_out = jnp.stack(bases[1:])
    return (bases_out, hessenberg, r_first)


def dot(a, b):
    return jnp.dot(a, b, preferred_element_type=F32)


def dot_rows(a, b, precision=None):
    return lax.dot_general(
        a, b, (((0,), (0,)), ((), ())), precision=precision, preferred_element_type=F32
    )


def rounded(x):
    return x.astype(BF16).astype(F32)


def split2(x):
    high = x.astype(BF16)
    return high, (x - high.astype(F32)).astype(BF16)


def both(x):
    return jnp.concatenate(split2(x), axis=1)


def square(x):
    pair = both(x)
    return jnp.concatenate([pair, pair], axis=0)


def halves(x):
    n = x.shape[1] // 2
    return x[:, :n] + x[:, n:]


def quarters(x):
    n = x.shape[0] // 2
    return halves(x[:n] + x[n:])


def kernel(
    dims,
    start_ref,
    diag_ref,
    blocks_ref,
    spans_ref,
    cols_ref,
    bases_ref,
    rest_ref,
    inverse_ref,
    hess_ref,
    first_ref,
    flag_ref,
    hess,
    first,
    blk,
    ext,
    qf,
    qs,
    mf,
    dg,
    work,
    fac,
    inv,
    spread,
    hb,
    lb,
    part,
    recv1,
    mid,
    recv2,
    fin,
    total,
    cond,
    send_sem,
    recv_sem,
    halo_send,
    halo_recv,
    blk_sem,
    out_sem,
):
    n_span, n_band, nb, bs, width, kc = dims
    n_xy, n_zc = n_span // 2, n_band * 2
    rows = nb * bs
    stride = nb + 2 * W
    chunk = width // n_xy
    scale = 1.0 / (rows * n_span * n_band)
    s = lax.axis_index("span")
    z = lax.axis_index("band")
    xy, core = s // 2, s % 2
    zc = z * 2 + core

    def xy_peer(d):
        peer = lax.rem(xy + d, n_xy)
        return peer, (peer * 2 + core, z)

    def zc_peer(d):
        peer = lax.rem(zc + d, n_zc)
        return peer, (xy * 2 + lax.rem(peer, 2), peer // 2)

    side = math.isqrt(n_xy)
    x, y = xy // side, xy % side

    def hops(step, count):
        return min(step, count - step)

    def xy_far(act):
        steps = [(dx, dy) for dx in range(side) for dy in range(side) if dx or dy]
        for dx, dy in sorted(steps, key=lambda t: -hops(t[0], side) - hops(t[1], side)):
            peer = lax.rem(x + dx, side) * side + lax.rem(y + dy, side)
            act((peer, (peer * 2 + core, z)))

    def zc_far(act):
        steps = [(dz, dc) for dz in range(n_band) for dc in range(2) if dz or dc]
        for dz, dc in sorted(steps, key=lambda t: -2 * hops(t[0], n_band) - t[1]):
            to_z, to_core = lax.rem(z + dz, n_band), lax.rem(core + dc, 2)
            act((to_z * 2 + to_core, (xy * 2 + to_core, to_z)))

    sibling, beyond = s + 1 - 2 * core, s - 1 + 2 * core
    has_beyond = (beyond >= 0) & (beyond < n_span)
    has_below, has_above = z > 0, z < n_band - 1
    near_seg, far_seg = (2 - 2 * core) * stride, 2 * core * stride
    always = z >= 0
    low, high = W, nb
    top = nb + W

    moves = [
        (stride + low, near_seg + low, W, (beyond, z), has_beyond, far_seg + low, has_beyond),
        (stride + high, near_seg + high, W, (beyond, z), has_beyond, far_seg + high, has_beyond),
        (stride + low, stride + top, W, (s, z - 1), has_below, stride + top, has_above),
        (stride + high, stride, W, (s, z + 1), has_above, stride, has_below),
        (stride + low, far_seg + low, nb, (sibling, z), always, near_seg + low, always),
        (
            stride + low + W,
            near_seg + low + W,
            nb - 2 * W,
            (beyond, z),
            has_beyond,
            far_seg + low + W,
            has_beyond,
        ),
        (stride, far_seg, W, (sibling, z), has_below, near_seg, has_below),
        (stride + top, far_seg + top, W, (sibling, z), has_above, near_seg + top, has_above),
        (
            far_seg + high,
            far_seg,
            W,
            (s, z + 1),
            has_beyond & has_above,
            far_seg,
            has_beyond & has_below,
        ),
        (
            far_seg + low,
            far_seg + top,
            W,
            (s, z - 1),
            has_beyond & has_below,
            far_seg + top,
            has_beyond & has_above,
        ),
    ]

    def move(n, source, target, count, device):
        return pltpu.make_async_remote_copy(
            src_ref=ext.at[pl.ds(source, count)],
            dst_ref=ext.at[pl.ds(target, count)],
            send_sem=halo_send.at[n],
            recv_sem=halo_recv.at[n],
            device_id=device,
            device_id_type=MESH,
        )

    def send(*chosen):
        for n in chosen:
            source, target, count, device, goes, _, _ = moves[n]

            @pl.when(goes)
            def _():
                move(n, source, target, count, device).start()

    def sent_halo(*chosen):
        for n in chosen:
            source, target, count, device, goes, _, _ = moves[n]

            @pl.when(goes)
            def _():
                move(n, source, target, count, device).wait_send()

    def arrived(*chosen):
        for n in chosen:
            source, _, count, device, _, here, comes = moves[n]

            @pl.when(comes)
            def _():
                move(n, source, here, count, device).wait_recv()

    first_load = pltpu.make_async_copy(start_ref, mf, blk_sem.at[0])
    first_load.start()
    load = pltpu.make_async_copy(blocks_ref, blk, blk_sem.at[1])
    barrier = pltpu.get_barrier_semaphore()

    def greet(peer_of):
        def body(d, carry):
            pl.semaphore_signal(barrier, inc=1, device_id=peer_of(d)[1], device_id_type=MESH)
            return carry

        return body

    lax.fori_loop(1, n_xy, greet(xy_peer), 0)
    lax.fori_loop(1, n_zc, greet(zc_peer), 0)

    @pl.when(has_beyond)
    def _():
        pl.semaphore_signal(barrier, inc=1, device_id=(beyond, z), device_id_type=MESH)

    load.start()

    def publish(t, bases):
        pair = both(mf[...])
        lefts = jnp.concatenate([qs[m] for m in range(bases)] + [pair], axis=1)
        value = dot_rows(lefts, pair).reshape(bases + 1, 2 * width, 2 * width)
        for m in range(bases + 1):
            part[t, :, m] = (quarters(value[m]) * scale).reshape(n_xy, chunk, width)

    def all_reduce(t, nm, meanwhile=None):
        take = pl.ds(0, nm)
        par = t % 2

        def copy(stage, source, target, device):
            return pltpu.make_async_remote_copy(
                src_ref=source,
                dst_ref=target,
                send_sem=send_sem.at[stage],
                recv_sem=recv_sem.at[par, stage],
                device_id=device,
                device_id_type=MESH,
            )

        def landed(stage, buffer, count):
            pieces = buffer.at[t, pl.ds(0, count - 1), take]
            copy(stage, pieces, pieces, (sibling, z)).wait_recv()

        def left(stage, buffer, count):
            pieces = buffer.at[t, pl.ds(0, count - 1), take]
            copy(stage, pieces, pieces, (sibling, z)).wait_send()

        xy_far(lambda who: copy(0, part.at[t, who[0], take], recv1.at[t, xy, take], who[1]).start())
        recv1[t, xy, :nm] = part[t, xy, :nm]
        if meanwhile is not None:
            meanwhile()
        landed(0, recv1, n_xy)
        value = recv1[t, 0, :nm]
        for i in range(1, n_xy):
            value = value + recv1[t, i, :nm]
        mid[t, :nm] = value
        zc_far(lambda who: copy(1, mid.at[t, take], recv2.at[t, zc, take], who[1]).start())
        recv2[t, zc, :nm] = value
        landed(1, recv2, n_zc)
        value = recv2[t, 0, :nm]
        for i in range(1, n_zc):
            value = value + recv2[t, i, :nm]
        fin[t, :nm] = value
        xy_far(lambda who: copy(2, fin.at[t, take], total.at[t, xy, take], who[1]).start())
        total[t, xy, :nm] = value
        landed(2, total, n_xy)

        def sent():
            left(0, recv1, n_xy)
            left(1, recv2, n_zc)
            left(2, total, n_xy)

        return [total[t, :, m].reshape(width, width) for m in range(nm)], sent

    def factor(matrix, beside):
        w = width
        tile = (8, w)
        work[:, :w] = matrix
        eye = lax.broadcasted_iota(jnp.int32, (w, w), 0) == lax.broadcasted_iota(
            jnp.int32, (w, w), 1
        )
        work[:, w:] = jnp.where(eye, 1.0, 0.0).astype(F32)
        row = lax.broadcasted_iota(jnp.int32, tile, 0)
        place = lax.broadcasted_iota(jnp.int32, (16, w), 0)
        lane = lax.broadcasted_iota(jnp.int32, (16, w), 1)
        lanes = lax.broadcasted_iota(jnp.int32, (w, w), 1)
        within, group = lax.rem(lanes, 16), lanes // 16
        firsts = (group == 0) | (group == 1) | (group == 4)
        seconds = (group == 2) | (group == 3)
        thirds = group == 5

        def assemble(lines):
            out = lines[7]
            for j in range(6, -1, -1):
                out = jnp.where(row == j, lines[j], out)
            return out

        def line(n, i):
            return jnp.broadcast_to(spread[n, pl.ds(i, 1), :], tile)

        def lines(n):
            return [line(n, i) for i in range(8)]

        def triangle(n):
            return [[line(n + j, i) if i >= j else None for j in range(8)] for i in range(8)]

        def eliminate(a, heads, tails, below):
            by = [None] * 8
            for j in range(8):
                by[j] = lax.rsqrt(a[j][j])
                heads[j] = heads[j] * by[j]
                tails[j] = tails[j] * by[j]
                for i in range(j + 1, 8):
                    a[i][j] = a[i][j] * by[j]
                if below:
                    below[j] = below[j] * by[j]
                for i in range(j + 1, 8):
                    for m in range(j + 1, i + 1):
                        a[i][m] = a[i][m] - a[i][j] * a[m][j]
                    heads[i] = heads[i] - a[i][j] * heads[j]
                    tails[i] = tails[i] - a[i][j] * tails[j]
                    if below:
                        below[i] = below[i] - below[j] * a[i][j]
            return by

        def substitute(a, by, heads, tails):
            for j in range(7, -1, -1):
                heads[j] = heads[j] * by[j]
                tails[j] = tails[j] * by[j]
                for i in range(j):
                    heads[i] = heads[i] - a[j][i] * heads[j]
                    tails[i] = tails[i] - a[j][i] * tails[j]

        def panel(p, carry):
            k0 = pl.multiple_of(p * 16, 16)
            upper = work[pl.ds(k0, 8), :w]
            lower = work[pl.ds(k0 + 8, 8), :w]

            def column(rows_of, j):
                return jnp.take_along_axis(rows_of, jnp.broadcast_to(k0 + j, tile), axis=1)

            for j in range(8):
                spread[j] = column(upper, j)
            below = [column(lower, j) for j in range(8)]
            block = [column(lower, 8 + j) for j in range(8)]
            spread[8] = upper
            spread[9] = work[pl.ds(k0, 8), w:]
            columns = jnp.take_along_axis(work[:, :w], k0 + within, axis=1)
            a1 = rounded(columns)
            a2 = rounded(columns - a1)
            a3 = columns - a1 - a2
            left = jnp.where(firsts, a1, jnp.where(seconds, a2, jnp.where(thirds, a3, 0.0)))
            left = left.astype(BF16)[:, :96]
            beside(p)
            a, heads, tails = triangle(0), lines(8), lines(9)
            by = eliminate(a, heads, tails, below)
            lower_tail = work[pl.ds(k0 + 8, 8), w:]
            for m in range(8):
                spread[10 + m] = below[m]
                lower = lower - below[m] * heads[m]
                lower_tail = lower_tail - below[m] * tails[m]
            cross = [[line(10 + m, i) for m in range(8)] for i in range(8)]
            for j in range(8):
                for m in range(8):
                    block[j] = block[j] - below[m] * cross[j][m]
                spread[18 + j] = block[j]
            spread[26] = lower
            spread[27] = lower_tail
            b, heads2, tails2 = triangle(18), lines(26), lines(27)
            by2 = eliminate(b, heads2, tails2, None)

            def stacked(first, second):
                return jnp.concatenate([assemble(first), assemble(second)], axis=0)

            fac[pl.ds(k0, 16), :] = jnp.where(lane >= k0 + place, stacked(heads, heads2), 0.0)
            inv[pl.ds(k0, 16), :] = stacked(tails, tails2)
            substitute(b, by2, heads2, tails2)
            for j in range(8):
                for i in range(7, -1, -1):
                    heads[j] = heads[j] - cross[i][j] * heads2[i]
                    tails[j] = tails[j] - cross[i][j] * tails2[i]
            substitute(a, by, heads, tails)
            right = jnp.concatenate([stacked(heads, heads2), stacked(tails, tails2)], axis=1)
            b1 = rounded(right)
            b2 = rounded(right - b1)
            b3 = right - b1 - b2
            rights = jnp.concatenate([b1, b2, b1, b2, b3, b1], axis=0).astype(BF16)
            work[...] = work[...] - dot(left, rights)
            return carry

        lax.fori_loop(0, w // 16, panel, 0)
        inverse = inv[...]
        lb[...] = square(inverse.T)
        diag = jnp.sum(jnp.where(eye, carry_gram[0], 0.0), axis=0, keepdims=True)
        cond[...] = cond[...] + diag * jnp.sum(inverse * inverse, axis=0, keepdims=True)

    carry_gram = [None]

    def form_basis(t):
        def form(i):
            here = pl.ds(pl.multiple_of(i * bs, bs), bs)
            q = halves(dot(both(mf[here, :]), lb[...]))
            qf[t, here, :] = q
            high, low = split2(q)
            qs[t, here, :] = jnp.concatenate([high, low], axis=1)
            ext[stride + W + i] = high

        def ends(e, carry):
            form(jnp.where(e < W, e, e + nb - 2 * W))
            return carry

        def middle(i, carry):
            form(i)
            return carry

        lax.fori_loop(0, 2 * W, ends, 0, unroll=True)
        send(0, 1, 2, 3)
        lax.fori_loop(W, nb - W, middle, 0, unroll=True)
        send(4, 5)

    cond[...] = jnp.zeros_like(cond)
    first_load.wait()
    publish(0, 0)
    pl.semaphore_wait(barrier, n_xy + n_zc - 2 + has_beyond.astype(jnp.int32))

    def expand_diag():
        ext[...] = jnp.zeros_like(ext)
        hess[...] = jnp.zeros_like(hess)

        def body(c, carry):
            line = jnp.broadcast_to(diag_ref[pl.ds(c, 1), :], (width, width))
            dg[pl.ds(pl.multiple_of(c * width, width), width), :] = line.T
            return carry

        lax.fori_loop(0, rows // width, body, 0)

    (matrix,), sent = all_reduce(0, 1, expand_diag)
    carry_gram[0] = matrix
    factor(matrix, lambda p: None)
    first[...] = fac[...]
    first_out = pltpu.make_async_copy(first, first_ref, out_sem.at[STEPS + 3])
    first_out.start()
    cut = rows - 2 * (rows // (width // 16))
    early_rows, late_rows = pl.ds(0, cut), pl.ds(cut, rows - cut)
    early = pltpu.make_async_copy(mf.at[early_rows], rest_ref.at[early_rows], out_sem.at[STEPS - 1])
    load.wait()

    for j in range(STEPS):
        form_basis(j)
        if j > 0:
            pltpu.make_async_copy(qf.at[j], bases_ref.at[j - 1], out_sem.at[j - 1]).start()
        sent()
        arrived(3)
        send(6)
        arrived(2)
        send(7)
        arrived(1)
        send(8)
        arrived(0)
        send(9)
        arrived(4, 5, 6, 7, 8, 9)

        def block_row(i, carry, j=j):
            here = pl.ds(pl.multiple_of(i * bs, bs), bs)
            acc = dg[here, :] * qf[j, here, :]
            for k in range(kc):
                at = (spans_ref[i, k] + 1) * stride + i + W + cols_ref[i, k]
                acc = acc + dot(blk[i, k], ext[at])
            mf[here, :] = acc
            return carry

        lax.fori_loop(0, nb, block_row, 0, unroll=4)
        sent_halo(6, 7, 8, 9)
        publish(j + 1, j + 1)
        sums, sent = all_reduce(j + 1, j + 2, lambda: sent_halo(0, 1, 2, 3, 4, 5))
        matrix = sums[j + 1]
        carry_gram[0] = matrix
        for i in range(j + 1):
            hess[i * width : (i + 1) * width, j * width : (j + 1) * width] = sums[i]
            hb[i] = square(sums[i])

        tallest = jnp.concatenate(sums[: j + 1], axis=0)
        matrix = matrix - dot_rows(tallest, tallest, HIGHEST)
        share = rows // (width // 16)

        def residual_part(p, j=j):
            here = pl.ds(pl.multiple_of(p * share, share), share)
            value = mf[here, :]
            for i in range(j + 1):
                value = value - halves(dot(qs[i, here, :], hb[i]))
            mf[here, :] = value
            if j == STEPS - 1:

                @pl.when(p == width // 16 - 2)
                def _():
                    early.start()

        factor(matrix, residual_part)
        hess[(j + 1) * width : (j + 2) * width, j * width : (j + 1) * width] = fac[...]

    ends = [
        pltpu.make_async_copy(mf.at[late_rows], rest_ref.at[late_rows], out_sem.at[STEPS]),
        pltpu.make_async_copy(lb, inverse_ref, out_sem.at[STEPS + 1]),
        pltpu.make_async_copy(hess, hess_ref, out_sem.at[STEPS + 2]),
    ]
    for copy in ends:
        copy.start()
    sent()
    flag_ref[0, 0] = jnp.sum(cond[...])
    for j in range(1, STEPS):
        pltpu.make_async_copy(qf.at[j], bases_ref.at[j - 1], out_sem.at[j - 1]).wait()
    early.wait()
    first_out.wait()
    for copy in ends:
        copy.wait()


def short_form(start_block, diagonal, blocks, span_offsets, col_offsets):
    n_span, n_band = lax.axis_size("span"), lax.axis_size("band")
    nb, kc, bs, _ = blocks.shape
    rows, width = start_block.shape
    dims = (n_span, n_band, nb, bs, width, kc)
    n_xy, n_zc = n_span // 2, n_band * 2
    stride = nb + 2 * W
    nm = STEPS + 1
    chunk = width // n_xy
    vmem = pl.BlockSpec(memory_space=pltpu.VMEM)
    smem = pl.BlockSpec(memory_space=pltpu.SMEM)
    anywhere = pl.BlockSpec(memory_space=pl.ANY)

    def body(*refs):
        kernel(dims, *refs)

    return pl.pallas_call(
        body,
        out_shape=(
            jax.ShapeDtypeStruct((STEPS - 1, rows, width), F32),
            jax.ShapeDtypeStruct((rows, width), F32),
            jax.ShapeDtypeStruct((2 * width, 2 * width), BF16),
            jax.ShapeDtypeStruct(((STEPS + 1) * width, STEPS * width), F32),
            jax.ShapeDtypeStruct((width, width), F32),
            jax.ShapeDtypeStruct((1, 1), F32),
        ),
        in_specs=[anywhere, vmem, anywhere, smem, smem],
        out_specs=(anywhere,) * 5 + (smem,),
        scratch_shapes=[
            pltpu.VMEM(((STEPS + 1) * width, STEPS * width), F32),
            pltpu.VMEM((width, width), F32),
            pltpu.VMEM((nb, kc, bs, bs), BF16),
            pltpu.VMEM((3 * stride, bs, width), BF16),
            pltpu.VMEM((STEPS, rows, width), F32),
            pltpu.VMEM((STEPS, rows, 2 * width), BF16),
            pltpu.VMEM((rows, width), F32),
            pltpu.VMEM((rows, width), F32),
            pltpu.VMEM((width, 2 * width), F32),
            pltpu.VMEM((width, width), F32),
            pltpu.VMEM((width, width), F32),
            pltpu.VMEM((28, 8, width), F32),
            pltpu.VMEM((STEPS, 2 * width, 2 * width), BF16),
            pltpu.VMEM((2 * width, 2 * width), BF16),
            pltpu.VMEM((nm, n_xy, nm, chunk, width), F32),
            pltpu.VMEM((nm, n_xy, nm, chunk, width), F32),
            pltpu.VMEM((nm, nm, chunk, width), F32),
            pltpu.VMEM((nm, n_zc, nm, chunk, width), F32),
            pltpu.VMEM((nm, nm, chunk, width), F32),
            pltpu.VMEM((nm, n_xy, nm, chunk, width), F32),
            pltpu.VMEM((1, width), F32),
            pltpu.SemaphoreType.DMA((3,)),
            pltpu.SemaphoreType.DMA((2, 3)),
            pltpu.SemaphoreType.DMA((10,)),
            pltpu.SemaphoreType.DMA((10,)),
            pltpu.SemaphoreType.DMA((2,)),
            pltpu.SemaphoreType.DMA((STEPS + 4,)),
        ],
        compiler_params=pltpu.CompilerParams(
            collective_id=0, has_side_effects=True, vmem_limit_bytes=48 * 1024 * 1024
        ),
    )(start_block, diagonal.reshape(rows // width, width), blocks, span_offsets, col_offsets)


def finish(bases, rest, inverse, hessenberg, r_first):
    before, rows, width = bases.shape
    chunks = 4
    chunk = rows // chunks

    def body(
        bases_ref, rest_ref, inverse_ref, hess_ref, first_ref, bases_to, hess_to, first_to, *scratch
    ):
        inv, q, r, out, hess, first, in_sem, out_sem = scratch
        fetch = pltpu.make_async_copy(inverse_ref, inv, in_sem.at[chunks + before + 2])
        fetch.start()
        parts = [pl.ds(i * chunk, chunk) for i in range(chunks)]
        loads = [
            pltpu.make_async_copy(rest_ref.at[here], r.at[here], in_sem.at[i])
            for i, here in enumerate(parts)
        ]
        others = [(bases_ref.at[i], q.at[i], bases_to.at[i]) for i in range(before)]
        others += [(hess_ref, hess, hess_to), (first_ref, first, first_to)]
        for i, (source, held, _) in enumerate(others):
            loads.append(pltpu.make_async_copy(source, held, in_sem.at[chunks + i]))
        for load in loads:
            load.start()
        stores = []
        fetch.wait()
        for i, here in enumerate(parts):
            loads[i].wait()
            out[here, :] = halves(dot(both(r[here, :]), inv[...]))
            stores.append(
                pltpu.make_async_copy(out.at[here], bases_to.at[before, here], out_sem.at[i])
            )
            stores[-1].start()
            if i < len(others):
                loads[chunks + i].wait()
                _, held, target = others[i]
                stores.append(pltpu.make_async_copy(held, target, out_sem.at[chunks + i]))
                stores[-1].start()
        for store in stores:
            store.wait()

    anywhere = pl.BlockSpec(memory_space=pl.ANY)
    return pl.pallas_call(
        body,
        out_shape=(
            jax.ShapeDtypeStruct((before + 1, rows, width), F32),
            jax.ShapeDtypeStruct(hessenberg.shape, F32),
            jax.ShapeDtypeStruct(r_first.shape, F32),
        ),
        in_specs=[anywhere] * 5,
        out_specs=(anywhere,) * 3,
        scratch_shapes=[
            pltpu.VMEM(inverse.shape, inverse.dtype),
            pltpu.VMEM(bases.shape, F32),
            pltpu.VMEM((rows, width), F32),
            pltpu.VMEM((rows, width), F32),
            pltpu.VMEM(hessenberg.shape, F32),
            pltpu.VMEM(r_first.shape, F32),
            pltpu.SemaphoreType.DMA((chunks + before + 3,)),
            pltpu.SemaphoreType.DMA((chunks + before + 2,)),
        ],
        compiler_params=pltpu.CompilerParams(vmem_limit_bytes=16 * 1024 * 1024),
    )(bases, rest, inverse, hessenberg, r_first)


def per_device(start_block, diagonal, blocks, span_offsets, col_offsets):
    args = (start_block, diagonal, blocks, span_offsets, col_offsets)
    *parts, spread = short_form(*args)
    return lax.cond(
        spread[0, 0] <= LIMIT,
        lambda: finish(*parts),
        lambda: plain_form(*args),
    )


def solution(mesh):
    placed = (
        P(("span", "band"), None),
        P(("span", "band")),
        P(("span", "band"), None, None, None),
        P(("span", "band"), None),
        P(("span", "band"), None),
    )
    return jax.shard_map(
        per_device,
        mesh=mesh,
        in_specs=placed,
        out_specs=(P(None, ("span", "band"), None), P(), P()),
        check_vma=False,
    )
```
